256 devices in a mesh: dp: 32 (over y, z_hi, x), mp: 8 (over z_lo, core).
Axes of the slice: x: 4, y: 4, z: 8 (z_hi: 2, z_lo: 4; z = z_hi * 4 + z_lo), core: 2. Of those that a mesh axis runs over, the one named last changes fastest.
Arguments:
- tokens: bfloat16 [2048, 6144], P('dp', 'mp'), may hold values from -60 to 60
- norm_gain: float32 [6144], P('mp'), may hold values from 0.5 to 1.5
- w_in: bfloat16 [6144, 24576], P('mp', 'dp'), may hold values from -0.078125 to 0.078125
- b_in: float32 [24576], P('dp'), may hold values from -4 to 4
- w_out: bfloat16 [24576, 6144], P('dp', 'mp'), may hold values from -0.0390625 to 0.0390625
- b_out: float32 [6144], P('mp'), may hold values from -3 to 3
- out_gain: float32 [6144], P('mp'), may hold values from 0.5 to 1.5
- student: bfloat16 [2048, 1024], P(('dp', 'mp')), may hold values from -45 to 45
- w_exit: bfloat16 [1024, 6144], P(None, 'mp'), may hold values from -0.1875 to 0.1875
Outputs:
- mean_loss: float32 [], replicated
- grad_exit: float32 [1024, 6144], P('dp', 'mp')
- grad_student: float32 [2048, 1024], P(('dp', 'mp'))
The draws below stay inside these ranges and needn't reach their ends.
All inputs are finite; a program needn't handle non-finite values.
Results may differ from the reference program's by a relative error of at most 0.0017.
Values may be sent and summed in bfloat16 or wider, within the bound.
A program may use at most 64 MiB of HBM per device.

```python
import jax
import jax.numpy as jnp
from jax import lax

D = 6144
FF = 24576
S = 1024
TOKENS = 2048


def draw_tokens(key, part):
    inner_key = jax.random.fold_in(key, 101)
    first_key, second_key, third_key = jax.random.split(inner_key, 3)
    rising = jnp.exp(jnp.log(3.0) * jnp.arange(D, dtype=jnp.float32) / (D - 1))
    column_scale = rising * jnp.exp(jax.random.uniform(second_key, (D,), jnp.float32, 0.0, jnp.log(3.3)))
    row_scale = 0.1 * jnp.exp(jax.random.uniform(third_key, (TOKENS, 1), jnp.float32, 0.0, jnp.log(10.0)))
    values = jnp.clip(jax.random.normal(first_key, (TOKENS, D), jnp.float32), -6.0, 6.0)
    return (values * row_scale * column_scale[None, :]).astype(jnp.bfloat16)


def draw_student(key, part):
    inner_key = jax.random.fold_in(key, 202)
    first_key, second_key = jax.random.split(inner_key, 2)
    rising = 1.0 + 2.0 * jnp.arange(TOKENS, dtype=jnp.float32) / (TOKENS - 1)
    column_scale = jnp.exp(jax.random.uniform(second_key, (S,), jnp.float32, 0.0, jnp.log(3.0)))
    values = jnp.clip(jax.random.normal(first_key, (TOKENS, S), jnp.float32), -5.0, 5.0)
    return (values * rising[:, None] * column_scale[None, :]).astype(jnp.bfloat16)


def block_scale(rng, extent, shards, least, largest):
    gain = 1.0
    for dim, shards_of in shards:
        draws = jax.random.uniform(jax.random.fold_in(jax.random.fold_in(rng, 6), dim), (shards_of,), jnp.float32, least / len(shards), largest / len(shards))
        gain = gain * jnp.repeat(jnp.exp(draws), extent[dim] // shards_of).reshape((-1,) + (1,) * (len(extent) - 1 - dim))
    return gain


def scatter_about(rng, dims, width, most, shards=(), held_as=jnp.bfloat16):
    array = jax.random.normal(rng, dims, jnp.float32) * width
    if len(shards) > 0:
        array = block_scale(rng, dims, shards, -0.22, 0.18) * array
    return jnp.clip(array, min=-most, max=most).astype(held_as)


def setup_inputs(seed: int = 0) -> dict:
    key_of = jax.random.split(jax.random.key(seed), 10)
    tokens = draw_tokens(jax.random.fold_in(key_of[9], 71), 0)
    norm_gain = jnp.clip(1.0 + 0.1 * jax.random.normal(key_of[1], (D,), jnp.float32), 0.5, 1.5)
    w_in = scatter_about(key_of[2], (D, FF), D ** -0.5, 0.078125, ((0, 8), (1, 32)))
    b_in = scatter_about(key_of[3], (FF,), 1.0, 4.0, ((0, 32),), jnp.float32)
    w_out = scatter_about(key_of[4], (FF, D), FF ** -0.5, 0.0390625, ((0, 32), (1, 8)))
    b_out = scatter_about(key_of[5], (D,), 0.5, 3.0, ((0, 8),), jnp.float32)
    out_gain = jnp.clip(1.0 + 0.1 * jax.random.normal(key_of[6], (D,), jnp.float32), 0.5, 1.5)
    student = draw_student(jax.random.fold_in(key_of[9], 71), 0)
    w_exit = scatter_about(key_of[8], (S, D), S ** -0.5, 0.1875, ((1, 8),))
    return {"tokens": tokens, "norm_gain": norm_gain, "w_in": w_in, "b_in": b_in, "w_out": w_out, "b_out": b_out, "out_gain": out_gain, "student": student, "w_exit": w_exit}


epsilon = 1e-06

def reference(tokens, norm_gain, w_in, b_in, w_out, b_out, out_gain, student, w_exit):
    inputs = tokens.astype(jnp.float32)
    scale_in = lax.rsqrt(lax.optimization_barrier(jnp.mean(inputs * inputs, axis=1, keepdims=True)) + epsilon)
    normed = (inputs * scale_in * norm_gain).astype(jnp.bfloat16)
    preact = jnp.dot(normed, w_in, preferred_element_type=jnp.float32) + b_in
    hidden = jax.nn.gelu(preact, approximate=False).astype(jnp.bfloat16)
    features = inputs + jnp.dot(hidden, w_out, preferred_element_type=jnp.float32) + b_out
    scale_out = lax.rsqrt(lax.optimization_barrier(jnp.mean(features * features, axis=1, keepdims=True)) + epsilon)
    target = features * scale_out * out_gain
    predicted = jnp.dot(student, w_exit, preferred_element_type=jnp.float32)
    errors = predicted - target
    mean_loss = jnp.mean(errors * errors)
    signal = (2.0 * errors).astype(jnp.bfloat16)
    grad_exit = jnp.dot(student.T, signal, preferred_element_type=jnp.float32) / TOKENS
    grad_student = jnp.dot(signal, w_exit.T, preferred_element_type=jnp.float32)
    return (mean_loss, grad_exit, grad_student)
```

```python
import math

import jax
import jax.numpy as jnp
from jax import lax
from jax.experimental import pallas as pl
from jax.experimental.pallas import tpu as pltpu
from jax.sharding import PartitionSpec as P

EPS = 1e-06
MESH = pl.DeviceIdType.MESH
F32, BF16 = jnp.float32, jnp.bfloat16

ROWS = 64
HALF = 32
FEAT = 768
HID = 768
STU = 1024
FEATURES = 6144
PATCHES = 2048
TILE = 256
CHUNKS = 8
LAG1, LAG2 = 1, 2


def dot(a, b):
    return jnp.dot(a, b, preferred_element_type=F32)


def kernel(
    tokens, norm_gain, w_in, b_in, w_out, b_out, out_gain, student, w_exit,
    loss_out, exit_out, student_out,
    w_in2, w_out2, w_exit2, vec, vec2, rows32, give, take, sq, xb, part, sent1, got1, hidden, sent2, got2,
    total, sent3, got3, sent4, got4, stu, stut, stua, pred, sig, siga, gstu, gotstu, gexit, gotg, gsum, gotz,
    l1, l2, l3, l4,
    s_core, r_core, s_sq, r_sq, s_x0, r_x0, s_st2, r_st2, s_zh, r_zh, s_rs, r_rs, s_ag, r_ag, s_p2, r_p2, s_p3, r_p3,
    s_stu, r_stu, s_sa, r_sa, s_sig, r_sig, s_gs, r_gs, s_gy, r_gy, s_gz, r_gz, s_l, r_l,
):
    d, m = lax.axis_index("dp"), lax.axis_index("mp")
    x, zh, y = d % 4, (d // 4) % 2, d // 8
    zl, c = m // 2, m % 2

    def at(yy, hh, xx, ll, cc):
        return ((yy * 2 + hh) * 4 + xx, ll * 2 + cc)

    def on_x(i, p=0):
        return at(y, zh, (x + i) % 4, zl, (c + p) % 2)

    def on_y(i):
        return at((y + i) % 4, zh, x, zl, c)

    def run_of(i):
        lo, hi = zl % 2, zl // 2
        lo = (lo + i % 2) % 2
        hi = (hi + i // 2) % 2
        return hi * 2 + lo

    def on_z(i):
        return at(y, zh, x, run_of(i), c)

    far = at(y, 1 - zh, x, zl, c)
    partner = at(y, zh, x, zl, 1 - c)

    def copy(src, dst, ss, rs, to):
        return pltpu.make_async_remote_copy(src, dst, ss, rs, device_id=to, device_id_type=MESH)

    bar = pltpu.get_barrier_semaphore()
    peers = [partner, far]
    for i in range(1, 4):
        peers += [on_x(i), on_x(i, 1), on_y(i), on_z(i)]
    for p in peers:
        pl.semaphore_signal(bar, 1, device_id=p, device_id_type=MESH)
    vec[0:1] = norm_gain[...]
    vec[1:2] = b_out[...]
    vec[2:3] = out_gain[...]
    vec[3:8] = jnp.zeros((5, FEAT), F32)
    rows32[...] = tokens[...].astype(F32).reshape(4, 2, 8, FEAT)
    give[...] = rows32[:, 1 - c].reshape(HALF, FEAT).astype(BF16)
    stu[zl] = student[...].astype(F32)
    pl.semaphore_wait(bar, len(peers))

    core_copies = [
        copy(src, dst, s_core.at[i], r_core.at[i], partner)
        for i, (src, dst) in enumerate(
            [(give, take), (vec, vec2), (w_in, w_in2), (w_out, w_out2), (w_exit, w_exit2)]
        )
    ]
    for cp in core_copies:
        cp.start()
    stu_copies = [copy(stu.at[zl], stu.at[zl], s_stu.at[i - 1], r_stu.at[i - 1], on_z(i)) for i in range(1, 4)]

    core_copies[0].wait_recv()
    own = rows32[:, c].reshape(HALF, FEAT)
    par = take[...].astype(F32)
    sq[0] = jnp.broadcast_to(
        jnp.sum(own * own, axis=1, keepdims=True) + jnp.sum(par * par, axis=1, keepdims=True), (HALF, 128)
    )
    sq_copies = [copy(sq.at[0], sq.at[i], s_sq.at[i - 1], r_sq.at[i - 1], on_z(i)) for i in range(1, 4)]
    for cp in sq_copies:
        cp.start()
    for cp in stu_copies:
        cp.start()
    core_copies[1].wait_recv()
    for cp in sq_copies:
        cp.wait_recv()
    ss = (sq[0] + sq[1]) + (sq[2] + sq[3])
    scale = lax.rsqrt(ss[:, 0:1] / FEATURES + EPS)
    xb[0, 0, 0, 0] = (own * scale * vec[0:1]).astype(BF16)
    xb[0, 0, 1, 0] = (par * scale * vec2[0:1]).astype(BF16)

    x0_copies = [
        copy(xb.at[0, 0, :, 0], xb.at[0, 0, :, 4 - i], s_x0.at[0, i - 1], r_x0.at[0, i - 1], on_x(i)) for i in range(1, 4)
    ]
    y0_copies = [
        copy(xb.at[1, 0, :, 0], xb.at[1, 0, :, 4 - i], s_x0.at[1, i - 1], r_x0.at[1, i - 1], on_y(i)) for i in range(1, 4)
    ]
    zh_copy = copy(xb.at[0, 0, :, 0], xb.at[1, 0, :, 0], s_zh.at[0], r_zh.at[0], far)
    zh_copy.start()
    for cp in x0_copies:
        cp.start()

    def stage2(dz, i):
        to = on_x(i) if dz else on_y(i)
        return copy(xb.at[dz, 0], xb.at[dz, 4 - i], s_st2.at[dz, i - 1], r_st2.at[dz, 4 - i - 1], to)

    zh_copy.wait_recv()
    for cp in y0_copies:
        cp.start()
    for cp in x0_copies:
        cp.wait_recv()
    for i in range(1, 4):
        stage2(0, i).start()
    for cp in y0_copies:
        cp.wait_recv()
    for i in range(1, 4):
        stage2(1, i).start()

    def rs_copy(k, i):
        return copy(sent1.at[k, run_of(i)], got1.at[k, i - 1], s_rs.at[k, i - 1], r_rs.at[k, i - 1], on_z(i))

    def ag_copy(k, i):
        return copy(hidden.at[k, zl], hidden.at[k, zl], s_ag.at[k, i - 1], r_ag.at[k, i - 1], on_z(i))

    def ag_wait(k, i):
        q = run_of(i)
        return copy(hidden.at[k, q], hidden.at[k, q], s_ag.at[k, i - 1], r_ag.at[k, i - 1], on_z(i))

    def p2_copy(dz, e, to):
        k = e * 2 + dz
        return copy(sent2.at[k - 2], got2.at[dz, e - 1], s_p2.at[dz, e - 1], r_p2.at[dz, e - 1], to)

    def p2_target(dz, e):
        return at((y + e * (1 - dz)) % 4, zh, (x + e * dz) % 4, zl, c)

    def first(k):
        dz, e = k % 2, k // 2

        @pl.when(e > 0)
        def _():
            copy(xb.at[dz, 0], xb.at[dz, e], s_st2.at[dz, e - 1], r_st2.at[dz, e - 1], partner).wait_recv()

        for t in range(HID // TILE):
            cols = slice(t * TILE, (t + 1) * TILE)
            a = dot(xb[dz, e, 0].reshape(4 * HALF, FEAT), w_in[:, cols])
            a += dot(xb[dz, e, 1].reshape(4 * HALF, FEAT), w_in2[:, cols])
            a = a.reshape(4, HALF, TILE)
            part[k, :, :, cols] = a
            sent1[k, :, :, cols] = a.astype(BF16)
        for i in range(1, 4):
            rs_copy(k, i).start()

    def middle(k):
        for i in range(1, 4):
            rs_copy(k, i).wait_recv()
        pre = part[k, zl] + b_in[...]
        pre += (got1[k, 0].astype(F32) + got1[k, 1].astype(F32)) + got1[k, 2].astype(F32)
        hidden[k, zl] = (0.5 * pre * (1.0 + lax.erf(pre * math.sqrt(0.5)))).astype(BF16)
        for i in range(1, 4):
            ag_copy(k, i).start()

    def second(k):
        dz, e = k % 2, k // 2
        for i in range(1, 4):
            ag_wait(k, i).wait_recv()
        h = hidden[k].reshape(4 * HALF, HID)
        for f, w in enumerate((w_out, w_out2)):
            for t in range(FEAT // TILE):
                cols = slice(t * TILE, (t + 1) * TILE)
                a = dot(h, w[:, cols]).reshape(4, HALF, TILE)

                @pl.when(e == 0)
                def _():
                    total[dz, f, :, :, cols] = a

                @pl.when(e > 0)
                def _():
                    sent2[k - 2, f, :, :, cols] = a.astype(BF16)

        @pl.when(e > 0)
        def _():
            p2_copy(dz, e, p2_target(dz, e)).start()

    core_copies[2].wait_recv()
    core_copies[3].wait_recv()

    def tick(t, carry):
        @pl.when(t < CHUNKS)
        def _():
            first(t)

        @pl.when((t >= LAG1) & (t < CHUNKS + LAG1))
        def _():
            middle(t - LAG1)

        @pl.when(t >= LAG2)
        def _():
            second(t - LAG2)

        return carry

    lax.fori_loop(0, CHUNKS + LAG2, tick, 0)

    for i in range(1, 4):
        q = run_of(i)
        copy(stu.at[q], stu.at[q], s_stu.at[i - 1], r_stu.at[i - 1], on_z(i)).wait_recv()
    learner = stu[...].reshape(HALF, STU).astype(BF16)
    stua[0, 0] = learner
    combos = [(i, p) for p in range(2) for i in range(4) if i or p]
    sa_copies = [
        copy(stua.at[0, 0], stua.at[(4 - i) % 4, p], s_sa.at[n], r_sa.at[n], on_x(i, p)) for n, (i, p) in enumerate(combos)
    ]
    for cp in sa_copies:
        cp.start()
    core_copies[4].wait_recv()
    for f, w in enumerate((w_exit, w_exit2)):
        for t in range(FEAT // TILE):
            cols = slice(t * TILE, (t + 1) * TILE)
            pred[f, :, cols] = dot(learner, w[:, cols])

    s2 = [None, None]
    p3 = [[None] * 3, [None] * 3]
    for dz in (1, 0):
        for i in range(3):
            p2_copy(dz, i + 1, partner).wait_recv()
        for s in range(3, -1, -1):
            a = total[dz, :, s] + got2[dz, 0, :, s].astype(F32)
            a += got2[dz, 1, :, s].astype(F32) + got2[dz, 2, :, s].astype(F32)
            if s == 0:
                total[dz, :, 0] = a
            else:
                sent3[dz, s - 1] = a.astype(BF16)
                p3[dz][s - 1] = copy(
                    sent3.at[dz, s - 1], got3.at[dz, s - 1], s_p3.at[dz, s - 1], r_p3.at[dz, s - 1],
                    on_y(s) if dz else on_x(s),
                )
                p3[dz][s - 1].start()
    for dz in (1, 0):
        for cp in p3[dz]:
            cp.wait_recv()
        a = total[dz, :, 0] + got3[dz, 0].astype(F32)
        a += got3[dz, 1].astype(F32) + got3[dz, 2].astype(F32)
        if dz:
            sent4[...] = a.astype(BF16)
            back = copy(sent4, got4, s_zh.at[1], r_zh.at[1], far)
            back.start()
        else:
            total[0, :, 0] = a

    for n, (i, p) in enumerate(combos):
        sa_copies[n].wait_recv()
    stut[...] = jnp.transpose(stua[...].reshape(8 * HALF, STU).astype(F32)).astype(BF16).reshape(8, 4, 32, 8 * HALF)

    back.wait_recv()
    sq2 = jnp.zeros((HALF, 1), F32)
    for f in range(2):
        v = vec if f == 0 else vec2
        inputs = rows32[:, c].reshape(HALF, FEAT) if f == 0 else take[...].astype(F32)
        a = inputs + (total[0, f, 0] + got4[f].astype(F32)) + v[1:2]
        total[1, f, 0] = a
        sq2 += jnp.sum(a * a, axis=1, keepdims=True)
    sq[4] = jnp.broadcast_to(sq2, (HALF, 128))
    sq2_copies = [copy(sq.at[4], sq.at[4 + i], s_sq.at[2 + i], r_sq.at[2 + i], on_z(i)) for i in range(1, 4)]
    for cp in sq2_copies:
        cp.start()
    for cp in sq2_copies:
        cp.wait_recv()
    ss = (sq[4] + sq[5]) + (sq[6] + sq[7])
    scale = lax.rsqrt(ss[:, 0:1] / FEATURES + EPS)
    loss = jnp.zeros((8, 128), F32)
    for f in (1, 0):
        v = vec if f == 0 else vec2
        err = pred[f] - total[1, f, 0] * scale * v[2:3]
        sig[f] = (2.0 * err).astype(BF16)
        es = jnp.sum((err * err).reshape(4, 8, FEAT), axis=0)
        for t in range(FEAT // 128):
            loss += es[:, t * 128 : (t + 1) * 128]
    siga[0, 0] = sig[0]

    sig_copies = [
        copy(sig.at[p], siga.at[(4 - i) % 4, p], s_sig.at[n], r_sig.at[n], on_x(i, p)) for n, (i, p) in enumerate(combos)
    ]
    for cp in sig_copies:
        cp.start()
    l1[zl] = loss
    l1_copies = [copy(l1.at[zl], l1.at[zl], s_l.at[i - 1], r_l.at[i - 1], on_z(i)) for i in range(1, 4)]
    for cp in l1_copies:
        cp.start()

    g = lax.dot_general(sig[0], w_exit[...], (((1,), (1,)), ((), ())), preferred_element_type=F32)
    g += lax.dot_general(sig[1], w_exit2[...], (((1,), (1,)), ((), ())), preferred_element_type=F32)
    gstu[...] = g.reshape(4, 8, STU)
    gs_copies = [
        copy(gstu.at[run_of(i)], gotstu.at[i - 1], s_gs.at[i - 1], r_gs.at[i - 1], on_z(i)) for i in range(1, 4)
    ]
    for cp in gs_copies:
        cp.start()

    for cp in sig_copies:
        cp.wait_recv()
    gexit[...] = dot(stut[:, x].reshape(8 * 32, 8 * HALF), siga[...].reshape(8 * HALF, FEAT)).reshape(4, 2, 32, FEAT)
    gy_copies = [
        copy(gexit.at[(y + i) % 4], gotg.at[i - 1], s_gy.at[i - 1], r_gy.at[i - 1], on_y(i)) for i in range(1, 4)
    ]
    for cp in gy_copies:
        cp.start()

    for i in range(1, 4):
        q = run_of(i)
        copy(l1.at[q], l1.at[q], s_l.at[i - 1], r_l.at[i - 1], on_z(i)).wait_recv()
    l2[x, c] = (l1[0] + l1[1]) + (l1[2] + l1[3])
    l2_copies = [copy(l2.at[x, c], l2.at[x, c], s_l.at[3 + n], r_l.at[3 + n], on_x(i, p)) for n, (i, p) in enumerate(combos)]
    for cp in l2_copies:
        cp.start()
    for cp in gs_copies:
        cp.wait_recv()
    student_out[...] = (gstu[zl] + gotstu[0]) + (gotstu[1] + gotstu[2])
    for n, (i, p) in enumerate(combos):
        xx, cc = (x + 4 - i) % 4, (c + p) % 2
        copy(l2.at[xx, cc], l2.at[xx, cc], s_l.at[3 + n], r_l.at[3 + n], partner).wait_recv()
    l3[y] = jnp.sum(l2[...].reshape(8, 8, 128), axis=0)
    l3_copies = [copy(l3.at[y], l3.at[y], s_l.at[9 + i], r_l.at[9 + i], on_y(i)) for i in range(1, 4)]
    for cp in l3_copies:
        cp.start()
    for cp in gy_copies:
        cp.wait_recv()
    gsum[...] = (gexit[y] + gotg[0]) + (gotg[1] + gotg[2])
    gz_copy = copy(gsum.at[1 - zh], gotz, s_gz.at[0], r_gz.at[0], far)
    gz_copy.start()
    for i in range(1, 4):
        yy = (y + 4 - i) % 4
        copy(l3.at[yy], l3.at[yy], s_l.at[9 + i], r_l.at[9 + i], partner).wait_recv()
    l4[zh] = (l3[0] + l3[1]) + (l3[2] + l3[3])
    l4_copy = copy(l4.at[zh], l4.at[zh], s_l.at[13], r_l.at[13], far)
    l4_copy.start()

    for cp in core_copies + stu_copies + sq_copies + x0_copies + y0_copies + [zh_copy, back]:
        cp.wait_send()
    for cp in sa_copies + p3[0] + p3[1] + sq2_copies + sig_copies + l1_copies + gs_copies + gy_copies + l2_copies + l3_copies:
        cp.wait_send()
    for dz in range(2):
        for i in range(1, 4):
            stage2(dz, i).wait_send()
            p2_copy(dz, i, partner).wait_send()

    def drain(k, carry):
        for i in range(1, 4):
            rs_copy(k, i).wait_send()
            ag_copy(k, i).wait_send()
        return carry

    lax.fori_loop(0, CHUNKS, drain, 0)

    copy(l4.at[1 - zh], l4.at[1 - zh], s_l.at[13], r_l.at[13], far).wait_recv()
    loss_out[0, 0] = jnp.sum(l4[0] + l4[1]) / (PATCHES * FEATURES)
    gz_copy.wait_recv()
    exit_out[...] = (gsum[zh] + gotz[...]) / PATCHES
    gz_copy.wait_send()
    l4_copy.wait_send()


def shards(tokens, norm_gain, w_in, b_in, w_out, b_out, out_gain, student, w_exit):
    vm = pltpu.VMEM
    dma = lambda *n: pltpu.SemaphoreType.DMA(n)
    in_vmem = pl.BlockSpec(memory_space=pltpu.VMEM)
    sems = []
    for shape in [(5,), (6,), (2, 3), (2, 3), (2,), (CHUNKS, 3), (CHUNKS, 3), (2, 3), (2, 3), (3,), (7,), (7,), (3,), (3,), (1,), (14,)]:
        sems += [dma(*shape), dma(*shape)]
    loss, g_exit, g_student = pl.pallas_call(
        kernel,
        out_shape=(
            jax.ShapeDtypeStruct((1, 1), F32),
            jax.ShapeDtypeStruct((32, FEAT), F32),
            jax.ShapeDtypeStruct((8, STU), F32),
        ),
        in_specs=[in_vmem] * 9,
        out_specs=(pl.BlockSpec(memory_space=pltpu.SMEM), in_vmem, in_vmem),
        scratch_shapes=[
            vm((FEAT, HID), BF16),
            vm((HID, FEAT), BF16),
            vm((STU, FEAT), BF16),
            vm((8, FEAT), F32),
            vm((8, FEAT), F32),
            vm((4, 2, 8, FEAT), F32),
            vm((HALF, FEAT), BF16),
            vm((HALF, FEAT), BF16),
            vm((8, HALF, 128), F32),
            vm((2, 4, 2, 4, HALF, FEAT), BF16),
            vm((CHUNKS, 4, HALF, HID), F32),
            vm((CHUNKS, 4, HALF, HID), BF16),
            vm((CHUNKS, 3, HALF, HID), BF16),
            vm((CHUNKS, 4, HALF, HID), BF16),
            vm((6, 2, 4, HALF, FEAT), BF16),
            vm((2, 3, 2, 4, HALF, FEAT), BF16),
            vm((2, 2, 4, HALF, FEAT), F32),
            vm((2, 3, 2, HALF, FEAT), BF16),
            vm((2, 3, 2, HALF, FEAT), BF16),
            vm((2, HALF, FEAT), BF16),
            vm((2, HALF, FEAT), BF16),
            vm((4, 8, STU), F32),
            vm((8, 4, 32, 8 * HALF), BF16),
            vm((4, 2, HALF, STU), BF16),
            vm((2, HALF, FEAT), F32),
            vm((2, HALF, FEAT), BF16),
            vm((4, 2, HALF, FEAT), BF16),
            vm((4, 8, STU), F32),
            vm((3, 8, STU), F32),
            vm((4, 2, 32, FEAT), F32),
            vm((3, 2, 32, FEAT), F32),
            vm((2, 32, FEAT), F32),
            vm((32, FEAT), F32),
            vm((4, 8, 128), F32),
            vm((4, 2, 8, 128), F32),
            vm((4, 8, 128), F32),
            vm((2, 8, 128), F32),
        ]
        + sems,
        compiler_params=pltpu.CompilerParams(
            collective_id=0, has_side_effects=True, vmem_limit_bytes=56 * 1024 * 1024
        ),
        name="branch_and_exit",
    )(
        tokens, norm_gain.reshape(1, FEAT), w_in, b_in.reshape(1, HID), w_out, b_out.reshape(1, FEAT),
        out_gain.reshape(1, FEAT), student, w_exit,
    )
    return loss.reshape(()), g_exit, g_student


def solution(mesh):
    placed = (
        P("dp", "mp"),
        P("mp"),
        P("mp", "dp"),
        P("dp"),
        P("dp", "mp"),
        P("mp"),
        P("mp"),
        P(("dp", "mp"), None),
        P(None, "mp"),
    )
    return jax.shard_map(
        shards,
        mesh=mesh,
        in_specs=placed,
        out_specs=(P(), P("dp", "mp"), P(("dp", "mp"), None)),
        check_vma=False,
    )
```

```python
import math

import jax
import jax.numpy as jnp
from jax import lax
from jax.experimental import pallas as pl
from jax.experimental.pallas import tpu as pltpu
from jax.sharding import PartitionSpec as P

EPS = 1e-06
MESH = pl.DeviceIdType.MESH
F32, BF16 = jnp.float32, jnp.bfloat16

ROWS = 64
HALF = 32
FEAT = 768
HID = 768
STU = 1024
FEATURES = 6144
PATCHES = 2048
SIDE = FEAT // 2
TILE = 256
CHUNKS = 8
LAG1, LAGF, LAG2 = 1, 2, 3
ORDER = ((0, 0), (1, 0), (0, 1), (1, 1), (1, 3), (1, 2), (0, 3), (0, 2))


def pick(n, table):
    v = table[0]
    for i in range(1, len(table)):
        v = jnp.where(n >= i, table[i], v)
    return v


def dot(a, b):
    return jnp.dot(a, b, preferred_element_type=F32)


def kernel(
    tokens, norm_gain, w_in, b_in, w_out, b_out, out_gain, student, w_exit,
    loss_out, exit_out, student_out,
    w_in2, w_out2, w_exit2, vec, vec2, rows32, give, mine, take, away, sq, xb, part, sent1, got1, hidden, sent2, got2,
    total, sent3, got3, sent4, got4, stu, stq, stut, stut1, stua, stub, pred, sig, sigs, siga, gstu, gotstu, gexit, gotg, gsum, gotz,
    l1, l2, l3, l4,
    s_core, r_core, s_sq, r_sq, s_x0, r_x0, s_st2, r_st2, s_zh, r_zh, s_rs, r_rs, s_ag, r_ag, s_p2, r_p2, s_p3, r_p3,
    s_stu, r_stu, s_sa, r_sa, s_sig, r_sig, s_gs, r_gs, s_gy, r_gy, s_gz, r_gz, s_l, r_l,
):
    d, m = lax.axis_index("dp"), lax.axis_index("mp")
    x, zh, y = d % 4, (d // 4) % 2, d // 8
    zl, c = m // 2, m % 2

    def at(yy, hh, xx, ll, cc):
        return ((yy * 2 + hh) * 4 + xx, ll * 2 + cc)

    def on_x(i, p=0):
        return at(y, zh, (x + i) % 4, zl, (c + p) % 2)

    def on_y(i, p=0):
        return at((y + i) % 4, zh, x, zl, (c + p) % 2)

    def on_ring(a, i, p=0):
        return on_y(i, p) if a else on_x(i, p)

    def run_of(i):
        lo, hi = zl % 2, zl // 2
        lo = (lo + i % 2) % 2
        hi = (hi + i // 2) % 2
        return hi * 2 + lo

    def on_z(i):
        return at(y, zh, x, run_of(i), c)

    far = at(y, 1 - zh, x, zl, c)
    partner = at(y, zh, x, zl, 1 - c)
    far_partner = at(y, 1 - zh, x, zl, 1 - c)

    def copy(src, dst, ss, rs, to):
        return pltpu.make_async_remote_copy(src, dst, ss, rs, device_id=to, device_id_type=MESH)

    bar = pltpu.get_barrier_semaphore()
    peers = [partner, far, far_partner]
    for i in range(1, 4):
        peers += [on_x(i), on_x(i, 1), on_y(i), on_y(i, 1), on_z(i)]
    for p in peers:
        pl.semaphore_signal(bar, 1, device_id=p, device_id_type=MESH)
    vec[0:1] = norm_gain[...].reshape(1, FEAT)
    vec[1:2] = b_out[...].reshape(1, FEAT)
    vec[2:3] = out_gain[...].reshape(1, FEAT)
    vec[3:8] = jnp.zeros((5, FEAT), F32)
    rows32[...] = tokens[...].astype(F32).reshape(4, 2, 8, FEAT)
    give[...] = rows32[:, 1 - c].reshape(HALF, FEAT).astype(BF16)
    mine[...] = rows32[:, c].reshape(HALF, FEAT).astype(BF16)
    stu[zl] = student[...].astype(F32)
    pl.semaphore_wait(bar, len(peers))

    core_copies = [
        copy(src, dst, s_core.at[i], r_core.at[i], partner)
        for i, (src, dst) in enumerate(
            [(give, take), (vec, vec2), (w_in, w_in2), (w_out, w_out2), (w_exit, w_exit2)]
        )
    ]
    far_copies = [
        copy(mine, away.at[0], s_zh.at[0], r_zh.at[0], far),
        copy(give, away.at[1], s_zh.at[1], r_zh.at[1], far_partner),
    ]
    for cp in core_copies[:2] + far_copies + core_copies[2:]:
        cp.start()
    stu_copies = [copy(stu.at[zl], stu.at[zl], s_stu.at[i - 1], r_stu.at[i - 1], on_z(i)) for i in range(1, 4)]

    def squares(n, u, v):
        sq[4 * n] = jnp.broadcast_to(
            jnp.sum(u * u, axis=1, keepdims=True) + jnp.sum(v * v, axis=1, keepdims=True), (HALF, 128)
        )
        cps = [copy(sq.at[4 * n], sq.at[4 * n + i], s_sq.at[n, i - 1], r_sq.at[n, i - 1], on_z(i)) for i in range(1, 4)]
        for cp in cps:
            cp.start()
        return cps

    def scale_of(n, cps):
        for cp in cps:
            cp.wait_recv()
        ss = (sq[4 * n] + sq[4 * n + 1]) + (sq[4 * n + 2] + sq[4 * n + 3])
        return lax.rsqrt(ss[:, 0:1] / FEATURES + EPS)

    core_copies[0].wait_recv()
    own = rows32[:, c].reshape(HALF, FEAT)
    par = take[...].astype(F32)
    sq_copies = squares(0, own, par)
    core_copies[1].wait_recv()
    scale = scale_of(0, sq_copies)
    xb[0, 0, 0, 0] = (own * scale * vec[0:1]).astype(BF16)
    xb[0, 0, 1, 0] = (par * scale * vec2[0:1]).astype(BF16)

    x0_copies = [
        copy(xb.at[0, 0, :, 0], xb.at[0, 0, :, 4 - i], s_x0.at[0, i - 1], r_x0.at[0, i - 1], on_x(i)) for i in range(1, 4)
    ]
    y0_copies = [
        copy(xb.at[1, 0, :, 0], xb.at[1, 0, :, 4 - i], s_x0.at[1, i - 1], r_x0.at[1, i - 1], on_y(i)) for i in range(1, 4)
    ]
    for cp in x0_copies:
        cp.start()
    for cp in far_copies:
        cp.wait_recv()
    own = away[0].astype(F32)
    par = away[1].astype(F32)
    sq1_copies = squares(1, own, par)
    scale = scale_of(1, sq1_copies)
    xb[1, 0, 0, 0] = (own * scale * vec[0:1]).astype(BF16)
    xb[1, 0, 1, 0] = (par * scale * vec2[0:1]).astype(BF16)
    for cp in y0_copies:
        cp.start()
    for cp in stu_copies:
        cp.start()

    def stage2(dz, i):
        to = on_x(i) if dz else on_y(i)
        return copy(xb.at[dz, 0], xb.at[dz, 4 - i], s_st2.at[dz, i - 1], r_st2.at[dz, 4 - i - 1], to)

    for cp in x0_copies:
        cp.wait_recv()
    for i in (1, 3):
        stage2(0, i).start()

    def rs_copy(k, i):
        return copy(sent1.at[k, run_of(i)], got1.at[k, i - 1], s_rs.at[k, i - 1], r_rs.at[k, i - 1], on_z(i))

    def ag_copy(k, i):
        q = run_of(2) if i == 3 else zl
        return copy(hidden.at[k, q], hidden.at[k, q], s_ag.at[k, i - 1], r_ag.at[k, i - 1], on_z(1 if i == 3 else i))

    def ag_wait(k, i):
        q = run_of(i)
        return copy(hidden.at[k, q], hidden.at[k, q], s_ag.at[k, i - 1], r_ag.at[k, i - 1], on_z(i))

    def p2_copy(dz, e, to):
        return copy(sent2.at[dz, e - 1], got2.at[dz, e - 1], s_p2.at[dz, e - 1], r_p2.at[dz, e - 1], to)

    def p2_target(dz, e):
        return at((y + e * (1 - dz)) % 4, zh, (x + e * dz) % 4, zl, c)

    def first(k):
        dz, e = pick(k, [n[0] for n in ORDER]), pick(k, [n[1] for n in ORDER])

        @pl.when(k == 1)
        def _():
            for cp in y0_copies:
                cp.wait_recv()
            for i in (1, 3):
                stage2(1, i).start()
            for dz in range(2):
                stage2(dz, 2).start()

        @pl.when(e > 0)
        def _():
            copy(xb.at[dz, 0], xb.at[dz, e], s_st2.at[dz, e - 1], r_st2.at[dz, e - 1], partner).wait_recv()

        for t in range(HID // TILE):
            cols = slice(t * TILE, (t + 1) * TILE)
            a = dot(xb[dz, e, 0].reshape(4 * HALF, FEAT), w_in[:, cols])
            a += dot(xb[dz, e, 1].reshape(4 * HALF, FEAT), w_in2[:, cols])
            a = a.reshape(4, HALF, TILE)
            part[k, :, :, cols] = a
            sent1[k, :, :, cols] = a.astype(BF16)
        for i in range(1, 4):
            rs_copy(k, i).start()

    def middle(k):
        for i in range(1, 4):
            rs_copy(k, i).wait_recv()
        pre = part[k, zl] + b_in[...].reshape(1, HID)
        pre += (got1[k, 0].astype(F32) + got1[k, 1].astype(F32)) + got1[k, 2].astype(F32)
        hidden[k, zl] = (0.5 * pre * (1.0 + lax.erf(pre * math.sqrt(0.5)))).astype(BF16)
        for i in (2, 1):
            ag_copy(k, i).start()

    def forward(k):
        ag_wait(k, 2).wait_recv()
        ag_copy(k, 3).start()

    def second(k):
        dz, e = pick(k, [n[0] for n in ORDER]), pick(k, [n[1] for n in ORDER])
        for i in (1, 3):
            ag_wait(k, i).wait_recv()
        h = hidden[k].reshape(4 * HALF, HID)
        for f, w in enumerate((w_out, w_out2)):
            for t in range(FEAT // TILE):
                cols = slice(t * TILE, (t + 1) * TILE)
                a = dot(h, w[:, cols]).reshape(4, HALF, TILE)

                @pl.when(e == 0)
                def _():
                    total[dz, f, :, :, cols] = a

                @pl.when(e > 0)
                def _():
                    sent2[dz, e - 1, f, :, :, cols] = a.astype(BF16)

        @pl.when(e > 0)
        def _():
            p2_copy(dz, e, p2_target(dz, e)).start()

    combos = [(i, p) for p in range(2) for i in range(4) if i or p]
    sa_copies = [
        copy(stua.at[0, 0], stua.at[(4 - i) % 4, p], s_sa.at[0, n], r_sa.at[0, n], on_x(i, p))
        for n, (i, p) in enumerate(combos)
    ]
    sa_copies += [
        copy(stq.at[(y + i) % 4], stub.at[(4 - i) % 4, p], s_sa.at[1, n], r_sa.at[1, n], on_y(i, p))
        for n, (i, p) in enumerate(combos)
    ]

    def gather_student():
        for i in range(1, 4):
            q = run_of(i)
            copy(stu.at[q], stu.at[q], s_stu.at[i - 1], r_stu.at[i - 1], on_z(i)).wait_recv()
        stua[0, 0] = stu[...].reshape(HALF, STU).astype(BF16)
        for i in range(4):
            stq[i] = stua[0, 0, :, i * 256 : (i + 1) * 256]
        stub[0, 0] = stq[y]
        for cp in sa_copies:
            cp.start()

    def predict():
        core_copies[4].wait_recv()
        for f, w in enumerate((w_exit, w_exit2)):
            for t in range(FEAT // TILE):
                cols = slice(t * TILE, (t + 1) * TILE)
                pred[f, :, cols] = dot(stua[0, 0], w[:, cols])

    def transpose_student():
        for cp in sa_copies:
            cp.wait_recv()
        stut1[...] = jnp.transpose(stub[...].reshape(8 * HALF, 256).astype(F32)).astype(BF16)
        stut[...] = jnp.transpose(stua[...].reshape(8 * HALF, STU).astype(F32)).astype(BF16).reshape(8, 4, 32, 8 * HALF)

    p3 = [
        [
            copy(
                sent3.at[dz, s - 1], got3.at[dz, s - 1], s_p3.at[dz, s - 1], r_p3.at[dz, s - 1],
                on_y(s) if dz else on_x(s),
            )
            for s in range(1, 4)
        ]
        for dz in range(2)
    ]
    back = copy(sent4, got4, s_zh.at[2], r_zh.at[2], far)

    def reduce2(dz):
        for i in range(3):
            p2_copy(dz, i + 1, partner).wait_recv()
        for s in (2, 1, 3, 0):
            a = total[dz, :, s] + got2[dz, 0, :, s].astype(F32)
            a += got2[dz, 1, :, s].astype(F32) + got2[dz, 2, :, s].astype(F32)
            if s == 0:
                total[dz, :, 0] = a
            else:
                sent3[dz, s - 1] = a.astype(BF16)
                p3[dz][s - 1].start()

    def reduce3(dz):
        for cp in p3[dz]:
            cp.wait_recv()
        a = total[dz, :, 0] + got3[dz, 0].astype(F32)
        a += got3[dz, 1].astype(F32) + got3[dz, 2].astype(F32)
        if dz:
            sent4[...] = a.astype(BF16)
            back.start()
        else:
            total[0, :, 0] = a

    core_copies[2].wait_recv()
    core_copies[3].wait_recv()

    def tick(t, carry):
        @pl.when(t < CHUNKS)
        def _():
            first(t)

        @pl.when((t >= LAG1) & (t < CHUNKS + LAG1))
        def _():
            middle(t - LAG1)

        @pl.when((t >= LAGF) & (t < CHUNKS + LAGF))
        def _():
            forward(t - LAGF)

        @pl.when(t >= LAG2)
        def _():
            second(t - LAG2)

        for when, what in ((2, gather_student), (3, predict), (5, transpose_student)):
            pl.when(t == when)(what)

        @pl.when(t == 9)
        def _():
            reduce2(1)

        return carry

    lax.fori_loop(0, CHUNKS + LAG2, tick, 0)
    reduce3(1)
    reduce2(0)
    reduce3(0)
    back.wait_recv()
    sq2 = jnp.zeros((HALF, 1), F32)
    for f in range(2):
        v = vec if f == 0 else vec2
        inputs = rows32[:, c].reshape(HALF, FEAT) if f == 0 else take[...].astype(F32)
        a = inputs + (total[0, f, 0] + got4[f].astype(F32)) + v[1:2]
        total[1, f, 0] = a
        sq2 += jnp.sum(a * a, axis=1, keepdims=True)
    sq[8] = jnp.broadcast_to(sq2, (HALF, 128))
    sq2_copies = [copy(sq.at[8], sq.at[8 + i], s_sq.at[2, i - 1], r_sq.at[2, i - 1], on_z(i)) for i in range(1, 4)]
    for cp in sq2_copies:
        cp.start()
    scale = scale_of(2, sq2_copies)
    loss = jnp.zeros((8, 128), F32)
    for f in (1, 0):
        v = vec if f == 0 else vec2
        err = pred[f] - total[1, f, 0] * scale * v[2:3]
        sig[f] = (2.0 * err).astype(BF16)
        for a in range(2):
            sigs[a, f] = sig[f, :, a * SIDE : (a + 1) * SIDE]
        es = jnp.sum((err * err).reshape(4, 8, FEAT), axis=0)
        for t in range(FEAT // 128):
            loss += es[:, t * 128 : (t + 1) * 128]
    for a in range(2):
        siga[a, 0, 0] = sigs[a, 0]

    sig_copies = [
        copy(sigs.at[a, p], siga.at[a, (4 - i) % 4, p], s_sig.at[a, n], r_sig.at[a, n], on_ring(a, i, p))
        for n, (i, p) in enumerate(combos)
        for a in range(2)
    ]
    for cp in sig_copies:
        cp.start()
    l1[zl] = loss
    l1_copies = [copy(l1.at[zl], l1.at[zl], s_l.at[i - 1], r_l.at[i - 1], on_z(i)) for i in range(1, 4)]
    for cp in l1_copies:
        cp.start()

    g = lax.dot_general(sig[0], w_exit[...], (((1,), (1,)), ((), ())), preferred_element_type=F32)
    g += lax.dot_general(sig[1], w_exit2[...], (((1,), (1,)), ((), ())), preferred_element_type=F32)
    gstu[...] = g.reshape(4, 8, STU)
    gs_copies = [
        copy(gstu.at[run_of(i)], gotstu.at[i - 1], s_gs.at[i - 1], r_gs.at[i - 1], on_z(i)) for i in range(1, 4)
    ]
    for cp in gs_copies:
        cp.start()

    for cp in sig_copies:
        cp.wait_recv()
    gexit[0] = dot(stut[:, x].reshape(256, 8 * HALF), siga[0].reshape(8 * HALF, SIDE)).reshape(4, 2, 32, SIDE)
    g = dot(stut1[...], siga[1].reshape(8 * HALF, SIDE)).reshape(2, 4, 32, SIDE)
    for h in range(2):
        gexit[1, :, h] = g[h]
    gy_copies = [
        copy(
            gexit.at[a, ((x if a else y) + i) % 4], gotg.at[a, i - 1], s_gy.at[a, i - 1], r_gy.at[a, i - 1],
            on_ring(1 - a, i),
        )
        for i in range(1, 4)
        for a in range(2)
    ]
    for cp in gy_copies:
        cp.start()

    for i in range(1, 4):
        q = run_of(i)
        copy(l1.at[q], l1.at[q], s_l.at[i - 1], r_l.at[i - 1], on_z(i)).wait_recv()
    l2[x, c] = (l1[0] + l1[1]) + (l1[2] + l1[3])
    l2_copies = [copy(l2.at[x, c], l2.at[x, c], s_l.at[3 + n], r_l.at[3 + n], on_x(i, p)) for n, (i, p) in enumerate(combos)]
    for cp in l2_copies:
        cp.start()
    for cp in gs_copies:
        cp.wait_recv()
    student_out[...] = (gstu[zl] + gotstu[0]) + (gotstu[1] + gotstu[2])
    for n, (i, p) in enumerate(combos):
        xx, cc = (x + 4 - i) % 4, (c + p) % 2
        copy(l2.at[xx, cc], l2.at[xx, cc], s_l.at[3 + n], r_l.at[3 + n], partner).wait_recv()
    l3[y] = jnp.sum(l2[...].reshape(8, 8, 128), axis=0)
    l3_copies = [copy(l3.at[y], l3.at[y], s_l.at[9 + i], r_l.at[9 + i], on_y(i)) for i in range(1, 4)]
    for cp in l3_copies:
        cp.start()
    for cp in gy_copies:
        cp.wait_recv()
    for a in range(2):
        gsum[:, a] = (gexit[a, x if a else y] + gotg[a, 0]) + (gotg[a, 1] + gotg[a, 2])
    gz_copy = copy(gsum.at[1 - zh], gotz, s_gz.at[0], r_gz.at[0], far)
    gz_copy.start()
    for i in range(1, 4):
        yy = (y + 4 - i) % 4
        copy(l3.at[yy], l3.at[yy], s_l.at[9 + i], r_l.at[9 + i], partner).wait_recv()
    l4[zh] = (l3[0] + l3[1]) + (l3[2] + l3[3])
    l4_copy = copy(l4.at[zh], l4.at[zh], s_l.at[13], r_l.at[13], far)
    l4_copy.start()

    for cp in core_copies + stu_copies + sq_copies + sq1_copies + x0_copies + y0_copies + far_copies + [back]:
        cp.wait_send()
    for cp in sa_copies + p3[0] + p3[1] + sq2_copies + sig_copies + l1_copies + gs_copies + gy_copies + l2_copies + l3_copies:
        cp.wait_send()
    for dz in range(2):
        for i in range(1, 4):
            stage2(dz, i).wait_send()
            p2_copy(dz, i, partner).wait_send()

    def drain(k, carry):
        for i in range(1, 4):
            rs_copy(k, i).wait_send()
            ag_copy(k, i).wait_send()
        return carry

    lax.fori_loop(0, CHUNKS, drain, 0)

    copy(l4.at[1 - zh], l4.at[1 - zh], s_l.at[13], r_l.at[13], far).wait_recv()
    loss_out[0, 0] = jnp.sum(l4[0] + l4[1]) / (PATCHES * FEATURES)
    gz_copy.wait_recv()
    for a in range(2):
        exit_out[:, a * SIDE : (a + 1) * SIDE] = (gsum[zh, a] + gotz[a]) / PATCHES
    gz_copy.wait_send()
    l4_copy.wait_send()


def shards(tokens, norm_gain, w_in, b_in, w_out, b_out, out_gain, student, w_exit):
    vm = pltpu.VMEM
    dma = lambda *n: pltpu.SemaphoreType.DMA(n)
    in_vmem = pl.BlockSpec(memory_space=pltpu.VMEM)
    sems = []
    for shape in [(5,), (3, 3), (2, 3), (2, 3), (3,), (CHUNKS, 3), (CHUNKS, 3), (2, 3), (2, 3), (3,), (2, 7), (2, 7), (3,), (2, 3), (1,), (14,)]:
        sems += [dma(*shape), dma(*shape)]
    loss, g_exit, g_student = pl.pallas_call(
        kernel,
        out_shape=(
            jax.ShapeDtypeStruct((1, 1), F32),
            jax.ShapeDtypeStruct((32, FEAT), F32),
            jax.ShapeDtypeStruct((8, STU), F32),
        ),
        in_specs=[in_vmem] * 9,
        out_specs=(pl.BlockSpec(memory_space=pltpu.SMEM), in_vmem, in_vmem),
        scratch_shapes=[
            vm((FEAT, HID), BF16),
            vm((HID, FEAT), BF16),
            vm((STU, FEAT), BF16),
            vm((8, FEAT), F32),
            vm((8, FEAT), F32),
            vm((4, 2, 8, FEAT), F32),
            vm((HALF, FEAT), BF16),
            vm((HALF, FEAT), BF16),
            vm((HALF, FEAT), BF16),
            vm((2, HALF, FEAT), BF16),
            vm((12, HALF, 128), F32),
            vm((2, 4, 2, 4, HALF, FEAT), BF16),
            vm((CHUNKS, 4, HALF, HID), F32),
            vm((CHUNKS, 4, HALF, HID), BF16),
            vm((CHUNKS, 3, HALF, HID), BF16),
            vm((CHUNKS, 4, HALF, HID), BF16),
            vm((2, 3, 2, 4, HALF, FEAT), BF16),
            vm((2, 3, 2, 4, HALF, FEAT), BF16),
            vm((2, 2, 4, HALF, FEAT), F32),
            vm((2, 3, 2, HALF, FEAT), BF16),
            vm((2, 3, 2, HALF, FEAT), BF16),
            vm((2, HALF, FEAT), BF16),
            vm((2, HALF, FEAT), BF16),
            vm((4, 8, STU), F32),
            vm((4, HALF, 256), BF16),
            vm((8, 4, 32, 8 * HALF), BF16),
            vm((256, 8 * HALF), BF16),
            vm((4, 2, HALF, STU), BF16),
            vm((4, 2, HALF, 256), BF16),
            vm((2, HALF, FEAT), F32),
            vm((2, HALF, FEAT), BF16),
            vm((2, 2, HALF, SIDE), BF16),
            vm((2, 4, 2, HALF, SIDE), BF16),
            vm((4, 8, STU), F32),
            vm((3, 8, STU), F32),
            vm((2, 4, 2, 32, SIDE), F32),
            vm((2, 3, 2, 32, SIDE), F32),
            vm((2, 2, 32, SIDE), F32),
            vm((2, 32, SIDE), F32),
            vm((4, 8, 128), F32),
            vm((4, 2, 8, 128), F32),
            vm((4, 8, 128), F32),
            vm((2, 8, 128), F32),
        ]
        + sems,
        compiler_params=pltpu.CompilerParams(
            collective_id=0, has_side_effects=True, vmem_limit_bytes=56 * 1024 * 1024
        ),
        name="branch_and_exit",
    )(
        tokens, norm_gain, w_in, b_in, w_out, b_out,
        out_gain, student, w_exit,
    )
    return loss.reshape(()), g_exit, g_student


def solution(mesh):
    placed = (
        P("dp", "mp"),
        P("mp"),
        P("mp", "dp"),
        P("dp"),
        P("dp", "mp"),
        P("mp"),
        P("mp"),
        P(("dp", "mp"), None),
        P(None, "mp"),
    )
    return jax.shard_map(
        shards,
        mesh=mesh,
        in_specs=placed,
        out_specs=(P(), P("dp", "mp"), P(("dp", "mp"), None)),
        check_vma=False,
    )
```

```python
import math

import jax
import jax.numpy as jnp
from jax import lax
from jax.experimental import pallas as pl
from jax.experimental.pallas import tpu as pltpu
from jax.sharding import PartitionSpec as P

EPS = 1e-06
MESH = pl.DeviceIdType.MESH
F32, BF16 = jnp.float32, jnp.bfloat16

ROWS = 64
HALF = 32
FEAT = 768
HID = 768
STU = 1024
FEATURES = 6144
PATCHES = 2048
SIDE = FEAT // 2
TILE = 256
CHUNKS = 8
LAG1, LAGF, LAG2, LAG3 = 1, 2, 3, 4
BACK = 10
ORDER = ((0, 0), (1, 0), (0, 1), (1, 1), (1, 3), (1, 2), (0, 3), (0, 2))


def pick(n, table):
    v = table[0]
    for i in range(1, len(table)):
        v = jnp.where(n >= i, table[i], v)
    return v


def dot(a, b):
    return jnp.dot(a, b, preferred_element_type=F32)


def kernel(
    tokens, norm_gain, w_in_hbm, b_in, w_out_hbm, b_out, out_gain, student, w_exit_hbm,
    loss_out, exit_out, student_out,
    w_in, w_out, w_exit, w_in2, w_out2, w_exit2, vec, vec2, rows32, give, mine, take, away, sq, xb, part, sent1, got1, hidden, sent2, got2,
    total, sent3, got3, sent4, got4, stu, stq, stut, stut1, stua, stub, pred, sig, sigs, siga, gstu, gotstu, gexit, gotg, gsum, gotz,
    l1, l2, l3, l4,
    s_load, s_core, r_core, s_sq, r_sq, s_x0, r_x0, s_st2, r_st2, s_zh, r_zh, s_rs, r_rs, s_ag, r_ag, s_p2, r_p2, s_p3, r_p3,
    s_stu, r_stu, s_sa, r_sa, s_sig, r_sig, s_gs, r_gs, s_gy, r_gy, s_gz, r_gz, s_l, r_l,
):
    d, m = lax.axis_index("dp"), lax.axis_index("mp")
    x, zh, y = d % 4, (d // 4) % 2, d // 8
    zl, c = m // 2, m % 2

    def at(yy, hh, xx, ll, cc):
        return ((yy * 2 + hh) * 4 + xx, ll * 2 + cc)

    def on_x(i, p=0):
        return at(y, zh, (x + i) % 4, zl, (c + p) % 2)

    def on_y(i, p=0):
        return at((y + i) % 4, zh, x, zl, (c + p) % 2)

    def on_ring(a, i, p=0):
        return on_y(i, p) if a else on_x(i, p)

    def run_of(i):
        lo, hi = zl % 2, zl // 2
        lo = (lo + i % 2) % 2
        hi = (hi + i // 2) % 2
        return hi * 2 + lo

    def on_z(i):
        return at(y, zh, x, run_of(i), c)

    far = at(y, 1 - zh, x, zl, c)
    partner = at(y, zh, x, zl, 1 - c)
    far_partner = at(y, 1 - zh, x, zl, 1 - c)

    def copy(src, dst, ss, rs, to):
        return pltpu.make_async_remote_copy(src, dst, ss, rs, device_id=to, device_id_type=MESH)

    bar = pltpu.get_barrier_semaphore()
    peers = [partner, far, far_partner]
    for i in range(1, 4):
        peers += [on_x(i), on_x(i, 1), on_y(i), on_y(i, 1), on_z(i)]
    for p in peers:
        pl.semaphore_signal(bar, 1, device_id=p, device_id_type=MESH)
    loads = [
        pltpu.make_async_copy(src, dst, s_load.at[i])
        for i, (src, dst) in enumerate([(w_in_hbm, w_in), (w_out_hbm, w_out), (w_exit_hbm, w_exit)])
    ]
    for cp in loads:
        cp.start()
    vec[0:1] = norm_gain[...].reshape(1, FEAT)
    vec[1:2] = b_out[...].reshape(1, FEAT)
    vec[2:3] = out_gain[...].reshape(1, FEAT)
    vec[3:8] = jnp.zeros((5, FEAT), F32)
    rows32[...] = tokens[...].astype(F32).reshape(4, 2, 8, FEAT)
    give[...] = rows32[:, 1 - c].reshape(HALF, FEAT).astype(BF16)
    mine[...] = rows32[:, c].reshape(HALF, FEAT).astype(BF16)
    stu[zl] = student[...].astype(F32)
    pl.semaphore_wait(bar, len(peers))

    core_copies = [
        copy(src, dst, s_core.at[i], r_core.at[i], partner)
        for i, (src, dst) in enumerate(
            [(give, take), (vec, vec2), (w_in, w_in2), (w_out, w_out2), (w_exit, w_exit2)]
        )
    ]
    far_copies = [
        copy(mine, away.at[0], s_zh.at[0], r_zh.at[0], far),
        copy(give, away.at[1], s_zh.at[1], r_zh.at[1], far_partner),
    ]
    for cp in core_copies[:2] + far_copies:
        cp.start()
    stu_copies = [copy(stu.at[zl], stu.at[zl], s_stu.at[i - 1], r_stu.at[i - 1], on_z(i)) for i in range(1, 4)]

    def squares(n, u, v):
        sq[4 * n] = jnp.broadcast_to(
            jnp.sum(u * u, axis=1, keepdims=True) + jnp.sum(v * v, axis=1, keepdims=True), (HALF, 128)
        )
        cps = [copy(sq.at[4 * n], sq.at[4 * n + i], s_sq.at[n, i - 1], r_sq.at[n, i - 1], on_z(i)) for i in range(1, 4)]
        for cp in cps:
            cp.start()
        return cps

    def scale_of(n, cps):
        for cp in cps:
            cp.wait_recv()
        ss = (sq[4 * n] + sq[4 * n + 1]) + (sq[4 * n + 2] + sq[4 * n + 3])
        return lax.rsqrt(ss[:, 0:1] / FEATURES + EPS)

    for i in range(3):
        loads[i].wait()
        core_copies[2 + i].start()
    core_copies[0].wait_recv()
    own = rows32[:, c].reshape(HALF, FEAT)
    par = take[...].astype(F32)
    sq_copies = squares(0, own, par)
    core_copies[1].wait_recv()
    scale = scale_of(0, sq_copies)
    xb[0, 0, 0, 0] = (own * scale * vec[0:1]).astype(BF16)
    xb[0, 0, 1, 0] = (par * scale * vec2[0:1]).astype(BF16)

    def stage1(dz, i):
        return copy(xb.at[dz, 0, :, 0], xb.at[dz, 4 - i, :, 0], s_x0.at[dz, i - 1], r_x0.at[dz, i - 1], on_ring(dz, i))

    def stage2(dz, s, i):
        to = at((y + i * (1 - dz)) % 4, zh, (x + i * dz) % 4, zl, c)
        return copy(xb.at[dz, s, :, 0], xb.at[dz, s, :, 4 - i], s_st2.at[dz, s, i - 1], r_st2.at[dz, s, i - 1], to)

    for dz in range(2):
        if dz:
            for cp in far_copies:
                cp.wait_recv()
            own = away[0].astype(F32)
            par = away[1].astype(F32)
            sq1_copies = squares(1, own, par)
            scale = scale_of(1, sq1_copies)
            xb[1, 0, 0, 0] = (own * scale * vec[0:1]).astype(BF16)
            xb[1, 0, 1, 0] = (par * scale * vec2[0:1]).astype(BF16)
        for i in (1, 3, 2):
            stage1(dz, i).start()
            stage2(dz, 0, i).start()
    for cp in stu_copies:
        cp.start()

    def pass_on(dz):
        for s in (1, 3, 2):
            stage1(dz, 4 - s).wait_recv()
            for i in (1, 3, 2):
                stage2(dz, s, i).start()

    pass_on(0)

    def rs_copy(k, i):
        return copy(sent1.at[k, run_of(i)], got1.at[k, i - 1], s_rs.at[k, i - 1], r_rs.at[k, i - 1], on_z(i))

    def ag_copy(k, i):
        q = run_of(2) if i == 3 else zl
        return copy(hidden.at[k, q], hidden.at[k, q], s_ag.at[k, i - 1], r_ag.at[k, i - 1], on_z(1 if i == 3 else i))

    def ag_wait(k, i):
        q = run_of(i)
        return copy(hidden.at[k, q], hidden.at[k, q], s_ag.at[k, i - 1], r_ag.at[k, i - 1], on_z(i))

    def p2_copy(dz, e, r):
        to = at((y + r * (1 - dz)) % 4, zh, (x + r * dz) % 4, zl, c)
        return copy(sent2.at[dz, e, r - 1], got2.at[dz, e, r - 1], s_p2.at[dz, e, r - 1], r_p2.at[dz, e, r - 1], to)

    def p3_copy(dz, e):
        to = at((y + e * dz) % 4, zh, (x + e * (1 - dz)) % 4, zl, c)
        return copy(sent3.at[dz, e - 1], got3.at[dz, e - 1], s_p3.at[dz, e - 1], r_p3.at[dz, e - 1], to)

    def place_of(k):
        return pick(k, [n[0] for n in ORDER]), pick(k, [n[1] for n in ORDER])

    def first(k):
        dz, e = place_of(k)

        @pl.when(k == 1)
        def _():
            pass_on(1)

        for r in range(1, 4):
            copy(xb.at[dz, e, :, r], xb.at[dz, e, :, r], s_st2.at[dz, e, 3 - r], r_st2.at[dz, e, 3 - r], partner).wait_recv()

        for t in range(HID // TILE):
            cols = slice(t * TILE, (t + 1) * TILE)
            a = dot(xb[dz, e, 0].reshape(4 * HALF, FEAT), w_in[:, cols])
            a += dot(xb[dz, e, 1].reshape(4 * HALF, FEAT), w_in2[:, cols])
            a = a.reshape(4, HALF, TILE)
            part[k, :, :, cols] = a
            sent1[k, :, :, cols] = a.astype(BF16)
        for i in range(1, 4):
            rs_copy(k, i).start()

    def middle(k):
        for i in range(1, 4):
            rs_copy(k, i).wait_recv()
        pre = part[k, zl] + b_in[...].reshape(1, HID)
        pre += (got1[k, 0].astype(F32) + got1[k, 1].astype(F32)) + got1[k, 2].astype(F32)
        hidden[k, zl] = (0.5 * pre * (1.0 + lax.erf(pre * math.sqrt(0.5)))).astype(BF16)
        for i in (2, 1):
            ag_copy(k, i).start()

    def forward(k):
        ag_wait(k, 2).wait_recv()
        ag_copy(k, 3).start()

    def second(k):
        dz, e = place_of(k)
        for i in (1, 3):
            ag_wait(k, i).wait_recv()
        h = hidden[k].reshape(4 * HALF, HID)
        for f, w in enumerate((w_out, w_out2)):
            for t in range(FEAT // TILE):
                cols = slice(t * TILE, (t + 1) * TILE)
                a = dot(h, w[:, cols]).reshape(4, HALF, TILE)
                total[dz, e, f, :, cols] = a[0]
                for r in range(1, 4):
                    sent2[dz, e, r - 1, f, :, cols] = a[r].astype(BF16)
        for r in (2, 1, 3):
            p2_copy(dz, e, r).start()

    def reduce2(k):
        dz, e = place_of(k)
        for r in range(1, 4):
            p2_copy(dz, e, r).wait_recv()
        a = (total[dz, e] + got2[dz, e, 0].astype(F32)) + (got2[dz, e, 1].astype(F32) + got2[dz, e, 2].astype(F32))

        @pl.when(e == 0)
        def _():
            total[dz, 0] = a

        @pl.when(e > 0)
        def _():
            sent3[dz, e - 1] = a.astype(BF16)
            p3_copy(dz, e).start()

    combos = [(i, p) for p in range(2) for i in range(4) if i or p]
    sa_copies = [
        copy(stua.at[0, 0], stua.at[(4 - i) % 4, p], s_sa.at[0, n], r_sa.at[0, n], on_x(i, p))
        for n, (i, p) in enumerate(combos)
    ]
    sa_copies += [
        copy(stq.at[(y + i) % 4], stub.at[(4 - i) % 4, p], s_sa.at[1, n], r_sa.at[1, n], on_y(i, p))
        for n, (i, p) in enumerate(combos)
    ]

    def gather_student():
        for i in range(1, 4):
            q = run_of(i)
            copy(stu.at[q], stu.at[q], s_stu.at[i - 1], r_stu.at[i - 1], on_z(i)).wait_recv()
        stua[0, 0] = stu[...].reshape(HALF, STU).astype(BF16)
        for i in range(4):
            stq[i] = stua[0, 0, :, i * 256 : (i + 1) * 256]
        stub[0, 0] = stq[y]
        for cp in sa_copies:
            cp.start()

    def predict():
        core_copies[4].wait_recv()
        for f, w in enumerate((w_exit, w_exit2)):
            for t in range(FEAT // TILE):
                cols = slice(t * TILE, (t + 1) * TILE)
                pred[f, :, cols] = dot(stua[0, 0], w[:, cols])

    def transpose_student():
        for cp in sa_copies:
            cp.wait_recv()
        stut1[...] = jnp.transpose(stub[...].reshape(8 * HALF, 256).astype(F32)).astype(BF16)
        stut[...] = jnp.transpose(stua[...].reshape(8 * HALF, STU).astype(F32)).astype(BF16).reshape(8, 4, 32, 8 * HALF)

    back = copy(sent4, got4, s_zh.at[2], r_zh.at[2], far)

    def reduce3(dz):
        for e in range(1, 4):
            p3_copy(dz, e).wait_recv()
        a = (total[dz, 0] + got3[dz, 0].astype(F32)) + (got3[dz, 1].astype(F32) + got3[dz, 2].astype(F32))
        if dz:
            sent4[...] = a.astype(BF16)
            back.start()
        else:
            total[0, 0] = a

    core_copies[2].wait_recv()
    core_copies[3].wait_recv()

    def tick(t, carry):
        @pl.when(t < CHUNKS)
        def _():
            first(t)

        @pl.when((t >= LAG1) & (t < CHUNKS + LAG1))
        def _():
            middle(t - LAG1)

        @pl.when((t >= LAGF) & (t < CHUNKS + LAGF))
        def _():
            forward(t - LAGF)

        @pl.when((t >= LAG2) & (t < CHUNKS + LAG2))
        def _():
            second(t - LAG2)

        @pl.when(t >= LAG3)
        def _():
            reduce2(t - LAG3)

        for when, what in ((2, gather_student), (3, predict), (5, transpose_student)):
            pl.when(t == when)(what)

        @pl.when(t == BACK)
        def _():
            reduce3(1)

        return carry

    lax.fori_loop(0, CHUNKS + LAG3, tick, 0)
    reduce3(0)
    back.wait_recv()
    sq2 = jnp.zeros((HALF, 1), F32)
    for f in range(2):
        v = vec if f == 0 else vec2
        inputs = rows32[:, c].reshape(HALF, FEAT) if f == 0 else take[...].astype(F32)
        a = inputs + (total[0, 0, f] + got4[f].astype(F32)) + v[1:2]
        total[1, 0, f] = a
        sq2 += jnp.sum(a * a, axis=1, keepdims=True)
    sq[8] = jnp.broadcast_to(sq2, (HALF, 128))
    sq2_copies = [copy(sq.at[8], sq.at[8 + i], s_sq.at[2, i - 1], r_sq.at[2, i - 1], on_z(i)) for i in range(1, 4)]
    for cp in sq2_copies:
        cp.start()
    scale = scale_of(2, sq2_copies)
    loss = jnp.zeros((8, 128), F32)
    for f in (1, 0):
        v = vec if f == 0 else vec2
        err = pred[f] - total[1, 0, f] * scale * v[2:3]
        sig[f] = (2.0 * err).astype(BF16)
        for a in range(2):
            sigs[a, f] = sig[f, :, a * SIDE : (a + 1) * SIDE]
        es = jnp.sum((err * err).reshape(4, 8, FEAT), axis=0)
        for t in range(FEAT // 128):
            loss += es[:, t * 128 : (t + 1) * 128]
    for a in range(2):
        siga[a, 0, 0] = sigs[a, 0]

    sig_copies = [
        copy(sigs.at[a, p], siga.at[a, (4 - i) % 4, p], s_sig.at[a, n], r_sig.at[a, n], on_ring(a, i, p))
        for n, (i, p) in enumerate(combos)
        for a in range(2)
    ]
    for cp in sig_copies:
        cp.start()
    l1[zl] = loss
    l1_copies = [copy(l1.at[zl], l1.at[zl], s_l.at[i - 1], r_l.at[i - 1], on_z(i)) for i in range(1, 4)]
    for cp in l1_copies:
        cp.start()

    g = lax.dot_general(sig[0], w_exit[...], (((1,), (1,)), ((), ())), preferred_element_type=F32)
    g += lax.dot_general(sig[1], w_exit2[...], (((1,), (1,)), ((), ())), preferred_element_type=F32)
    gstu[...] = g.reshape(4, 8, STU)
    gs_copies = [
        copy(gstu.at[run_of(i)], gotstu.at[i - 1], s_gs.at[i - 1], r_gs.at[i - 1], on_z(i)) for i in range(1, 4)
    ]
    for cp in gs_copies:
        cp.start()

    for cp in sig_copies:
        cp.wait_recv()
    gexit[0] = dot(stut[:, x].reshape(256, 8 * HALF), siga[0].reshape(8 * HALF, SIDE)).reshape(4, 2, 32, SIDE)
    g = dot(stut1[...], siga[1].reshape(8 * HALF, SIDE)).reshape(2, 4, 32, SIDE)
    for h in range(2):
        gexit[1, :, h] = g[h]
    gy_copies = [
        copy(
            gexit.at[a, ((x if a else y) + i) % 4], gotg.at[a, i - 1], s_gy.at[a, i - 1], r_gy.at[a, i - 1],
            on_ring(1 - a, i),
        )
        for i in range(1, 4)
        for a in range(2)
    ]
    for cp in gy_copies:
        cp.start()

    for i in range(1, 4):
        q = run_of(i)
        copy(l1.at[q], l1.at[q], s_l.at[i - 1], r_l.at[i - 1], on_z(i)).wait_recv()
    l2[x, c] = (l1[0] + l1[1]) + (l1[2] + l1[3])
    l2_copies = [copy(l2.at[x, c], l2.at[x, c], s_l.at[3 + n], r_l.at[3 + n], on_x(i, p)) for n, (i, p) in enumerate(combos)]
    for cp in l2_copies:
        cp.start()
    for cp in gs_copies:
        cp.wait_recv()
    student_out[...] = (gstu[zl] + gotstu[0]) + (gotstu[1] + gotstu[2])
    for n, (i, p) in enumerate(combos):
        xx, cc = (x + 4 - i) % 4, (c + p) % 2
        copy(l2.at[xx, cc], l2.at[xx, cc], s_l.at[3 + n], r_l.at[3 + n], partner).wait_recv()
    l3[y] = jnp.sum(l2[...].reshape(8, 8, 128), axis=0)
    l3_copies = [copy(l3.at[y], l3.at[y], s_l.at[9 + i], r_l.at[9 + i], on_y(i)) for i in range(1, 4)]
    for cp in l3_copies:
        cp.start()
    for cp in gy_copies:
        cp.wait_recv()
    for a in range(2):
        gsum[:, a] = (gexit[a, x if a else y] + gotg[a, 0]) + (gotg[a, 1] + gotg[a, 2])
    gz_copy = copy(gsum.at[1 - zh], gotz, s_gz.at[0], r_gz.at[0], far)
    gz_copy.start()
    for i in range(1, 4):
        yy = (y + 4 - i) % 4
        copy(l3.at[yy], l3.at[yy], s_l.at[9 + i], r_l.at[9 + i], partner).wait_recv()
    l4[zh] = (l3[0] + l3[1]) + (l3[2] + l3[3])
    l4_copy = copy(l4.at[zh], l4.at[zh], s_l.at[13], r_l.at[13], far)
    l4_copy.start()

    for cp in core_copies + stu_copies + sq_copies + sq1_copies + far_copies + [back]:
        cp.wait_send()
    for cp in sa_copies + sq2_copies + sig_copies + l1_copies + gs_copies + gy_copies + l2_copies + l3_copies:
        cp.wait_send()
    for dz in range(2):
        for i in range(1, 4):
            stage1(dz, i).wait_send()
            p3_copy(dz, i).wait_send()

    def drain(k, carry):
        for i in range(1, 4):
            rs_copy(k, i).wait_send()
            ag_copy(k, i).wait_send()
            stage2(k // 4, k % 4, i).wait_send()
            p2_copy(k // 4, k % 4, i).wait_send()
        return carry

    lax.fori_loop(0, CHUNKS, drain, 0)

    copy(l4.at[1 - zh], l4.at[1 - zh], s_l.at[13], r_l.at[13], far).wait_recv()
    loss_out[0, 0] = jnp.sum(l4[0] + l4[1]) / (PATCHES * FEATURES)
    gz_copy.wait_recv()
    for a in range(2):
        exit_out[:, a * SIDE : (a + 1) * SIDE] = (gsum[zh, a] + gotz[a]) / PATCHES
    gz_copy.wait_send()
    l4_copy.wait_send()


def place(a, b, a_out, b_out):
    a_out[...] = a[...]
    b_out[...] = b[...]


def shards(tokens, norm_gain, w_in, b_in, w_out, b_out, out_gain, student, w_exit):
    vm = pltpu.VMEM
    dma = lambda *n: pltpu.SemaphoreType.DMA(n)
    in_vmem = pl.BlockSpec(memory_space=pltpu.VMEM)
    in_hbm = pl.BlockSpec(memory_space=pl.ANY)
    sems = [dma(3)]
    for shape in [(5,), (3, 3), (2, 3), (2, 4, 3), (3,), (CHUNKS, 3), (CHUNKS, 3), (2, 4, 3), (2, 3), (3,), (2, 7), (2, 7), (3,), (2, 3), (1,), (14,)]:
        sems += [dma(*shape), dma(*shape)]
    loss, g_exit, g_student = pl.pallas_call(
        kernel,
        out_shape=(
            jax.ShapeDtypeStruct((1, 1), F32),
            jax.ShapeDtypeStruct((32, FEAT), F32),
            jax.ShapeDtypeStruct((8, STU), F32),
        ),
        in_specs=[in_vmem, in_vmem, in_hbm, in_vmem, in_hbm, in_vmem, in_vmem, in_vmem, in_hbm],
        out_specs=(pl.BlockSpec(memory_space=pltpu.SMEM), in_vmem, in_vmem),
        scratch_shapes=[
            vm((FEAT, HID), BF16),
            vm((HID, FEAT), BF16),
            vm((STU, FEAT), BF16),
            vm((FEAT, HID), BF16),
            vm((HID, FEAT), BF16),
            vm((STU, FEAT), BF16),
            vm((8, FEAT), F32),
            vm((8, FEAT), F32),
            vm((4, 2, 8, FEAT), F32),
            vm((HALF, FEAT), BF16),
            vm((HALF, FEAT), BF16),
            vm((HALF, FEAT), BF16),
            vm((2, HALF, FEAT), BF16),
            vm((12, HALF, 128), F32),
            vm((2, 4, 2, 4, HALF, FEAT), BF16),
            vm((CHUNKS, 4, HALF, HID), F32),
            vm((CHUNKS, 4, HALF, HID), BF16),
            vm((CHUNKS, 3, HALF, HID), BF16),
            vm((CHUNKS, 4, HALF, HID), BF16),
            vm((2, 4, 3, 2, HALF, FEAT), BF16),
            vm((2, 4, 3, 2, HALF, FEAT), BF16),
            vm((2, 4, 2, HALF, FEAT), F32),
            vm((2, 3, 2, HALF, FEAT), BF16),
            vm((2, 3, 2, HALF, FEAT), BF16),
            vm((2, HALF, FEAT), BF16),
            vm((2, HALF, FEAT), BF16),
            vm((4, 8, STU), F32),
            vm((4, HALF, 256), BF16),
            vm((8, 4, 32, 8 * HALF), BF16),
            vm((256, 8 * HALF), BF16),
            vm((4, 2, HALF, STU), BF16),
            vm((4, 2, HALF, 256), BF16),
            vm((2, HALF, FEAT), F32),
            vm((2, HALF, FEAT), BF16),
            vm((2, 2, HALF, SIDE), BF16),
            vm((2, 4, 2, HALF, SIDE), BF16),
            vm((4, 8, STU), F32),
            vm((3, 8, STU), F32),
            vm((2, 4, 2, 32, SIDE), F32),
            vm((2, 3, 2, 32, SIDE), F32),
            vm((2, 2, 32, SIDE), F32),
            vm((2, 32, SIDE), F32),
            vm((4, 8, 128), F32),
            vm((4, 2, 8, 128), F32),
            vm((4, 8, 128), F32),
            vm((2, 8, 128), F32),
        ]
        + sems,
        compiler_params=pltpu.CompilerParams(
            collective_id=0, has_side_effects=True, vmem_limit_bytes=56 * 1024 * 1024
        ),
        name="branch_and_exit",
    )(
        tokens, norm_gain, w_in, b_in, w_out, b_out,
        out_gain, student, w_exit,
    )
    g_exit, g_student = pl.pallas_call(
        place,
        out_shape=(jax.ShapeDtypeStruct((32, FEAT), F32), jax.ShapeDtypeStruct((8, STU), F32)),
        in_specs=[in_vmem] * 2,
        out_specs=(in_vmem, in_vmem),
        name="place",
    )(g_exit, g_student)
    return loss.reshape(()), g_exit, g_student


def solution(mesh):
    placed = (
        P("dp", "mp"),
        P("mp"),
        P("mp", "dp"),
        P("dp"),
        P("dp", "mp"),
        P("mp"),
        P("mp"),
        P(("dp", "mp"), None),
        P(None, "mp"),
    )
    return jax.shard_map(
        shards,
        mesh=mesh,
        in_specs=placed,
        out_specs=(P(), P("dp", "mp"), P(("dp", "mp"), None)),
        check_vma=False,
    )
```

```python
import math

import jax
import jax.numpy as jnp
from jax import lax
from jax.experimental import pallas as pl
from jax.experimental.pallas import tpu as pltpu
from jax.sharding import PartitionSpec as P

EPS = 1e-06
MESH = pl.DeviceIdType.MESH
F32, BF16 = jnp.float32, jnp.bfloat16

ROWS = 64
HALF = 32
FEAT = 768
HID = 768
STU = 1024
FEATURES = 6144
PATCHES = 2048
SIDE = FEAT // 2
TILE = 256
CHUNKS = 8
LAG1, LAGF, LAG2, LAG3 = 1, 2, 3, 4
BACK = 10
ORDER = ((0, 0), (1, 0), (1, 1), (1, 3), (0, 1), (1, 2), (0, 3), (0, 2))


def pick(n, table):
    v = table[0]
    for i in range(1, len(table)):
        v = jnp.where(n >= i, table[i], v)
    return v


def dot(a, b):
    return jnp.dot(a, b, preferred_element_type=F32)


def kernel(
    tokens, norm_gain, w_in_hbm, b_in, w_out_hbm, b_out, out_gain, student, w_exit_hbm,
    loss_out, exit_out, student_out,
    w_in, w_out, w_exit, w_in2, w_out2, w_exit2, vec, vec2, rows32, give, mine, take, away, sq, xb, part, sent1, got1, hidden, sent2, got2,
    total, sent3, got3, sent4, got4, stu, stq, stut, stut1, stua, stub, pred, sig, sigs, siga, gstu, gotstu, gexit, gotg, gsum, gotz,
    l1, l2, l3, l4,
    s_load, s_core, r_core, s_sq, r_sq, s_x0, r_x0, s_st2, r_st2, s_zh, r_zh, s_rs, r_rs, s_ag, r_ag, s_p2, r_p2, s_p3, r_p3,
    s_stu, r_stu, s_sa, r_sa, s_sig, r_sig, s_gs, r_gs, s_gy, r_gy, s_gz, r_gz, s_l, r_l,
):
    d, m = lax.axis_index("dp"), lax.axis_index("mp")
    x, zh, y = d % 4, (d // 4) % 2, d // 8
    zl, c = m // 2, m % 2

    def at(yy, hh, xx, ll, cc):
        return ((yy * 2 + hh) * 4 + xx, ll * 2 + cc)

    def on_x(i, p=0):
        return at(y, zh, (x + i) % 4, zl, (c + p) % 2)

    def on_y(i, p=0):
        return at((y + i) % 4, zh, x, zl, (c + p) % 2)

    def on_ring(a, i, p=0):
        return on_y(i, p) if a else on_x(i, p)

    def run_of(i):
        lo, hi = zl % 2, zl // 2
        lo = (lo + i % 2) % 2
        hi = (hi + i // 2) % 2
        return hi * 2 + lo

    def on_z(i):
        return at(y, zh, x, run_of(i), c)

    far = at(y, 1 - zh, x, zl, c)
    partner = at(y, zh, x, zl, 1 - c)
    far_partner = at(y, 1 - zh, x, zl, 1 - c)

    def copy(src, dst, ss, rs, to):
        return pltpu.make_async_remote_copy(src, dst, ss, rs, device_id=to, device_id_type=MESH)

    bar = pltpu.get_barrier_semaphore()
    peers = [partner, far, far_partner]
    for i in range(1, 4):
        peers += [on_x(i), on_x(i, 1), on_y(i), on_y(i, 1), on_z(i)]
    for p in peers:
        pl.semaphore_signal(bar, 1, device_id=p, device_id_type=MESH)
    loads = [
        pltpu.make_async_copy(src, dst, s_load.at[i])
        for i, (src, dst) in enumerate([(w_in_hbm, w_in), (w_out_hbm, w_out), (w_exit_hbm, w_exit)])
    ]
    for cp in loads:
        cp.start()
    vec[0:1] = norm_gain[...].reshape(1, FEAT)
    vec[1:2] = b_out[...].reshape(1, FEAT)
    vec[2:3] = out_gain[...].reshape(1, FEAT)
    vec[3:8] = jnp.zeros((5, FEAT), F32)
    rows32[...] = tokens[...].astype(F32).reshape(4, 2, 8, FEAT)
    give[...] = rows32[:, 1 - c].reshape(HALF, FEAT).astype(BF16)
    mine[...] = rows32[:, c].reshape(HALF, FEAT).astype(BF16)
    stu[zl] = student[...].astype(F32)
    pl.semaphore_wait(bar, len(peers))

    core_copies = [
        copy(src, dst, s_core.at[i], r_core.at[i], partner)
        for i, (src, dst) in enumerate(
            [(give, take), (vec, vec2), (w_in, w_in2), (w_out, w_out2), (w_exit, w_exit2)]
        )
    ]
    far_copies = [
        copy(mine, away.at[0], s_zh.at[0], r_zh.at[0], far),
        copy(give, away.at[1], s_zh.at[1], r_zh.at[1], far_partner),
    ]
    for cp in core_copies[:2] + far_copies:
        cp.start()
    stu_copies = [copy(stu.at[zl], stu.at[zl], s_stu.at[i - 1], r_stu.at[i - 1], on_z(i)) for i in range(1, 4)]

    def squares(n, u, v):
        sq[4 * n] = jnp.broadcast_to(
            jnp.sum(u * u, axis=1, keepdims=True) + jnp.sum(v * v, axis=1, keepdims=True), (HALF, 128)
        )
        cps = [copy(sq.at[4 * n], sq.at[4 * n + i], s_sq.at[n, i - 1], r_sq.at[n, i - 1], on_z(i)) for i in range(1, 4)]
        for cp in cps:
            cp.start()
        return cps

    def scale_of(n, cps):
        for cp in cps:
            cp.wait_recv()
        ss = (sq[4 * n] + sq[4 * n + 1]) + (sq[4 * n + 2] + sq[4 * n + 3])
        return lax.rsqrt(ss[:, 0:1] / FEATURES + EPS)

    for i in range(3):
        loads[i].wait()
        core_copies[2 + i].start()
    core_copies[0].wait_recv()
    own = rows32[:, c].reshape(HALF, FEAT)
    par = take[...].astype(F32)
    sq_copies = squares(0, own, par)
    core_copies[1].wait_recv()
    scale = scale_of(0, sq_copies)
    xb[0, 0, 0, 0] = (own * scale * vec[0:1]).astype(BF16)
    xb[0, 0, 1, 0] = (par * scale * vec2[0:1]).astype(BF16)

    def stage1(dz, i):
        return copy(xb.at[dz, 0, :, 0], xb.at[dz, 4 - i, :, 0], s_x0.at[dz, i - 1], r_x0.at[dz, i - 1], on_ring(dz, i))

    def stage2(dz, s, i):
        to = at((y + i * (1 - dz)) % 4, zh, (x + i * dz) % 4, zl, c)
        return copy(xb.at[dz, s, :, 0], xb.at[dz, s, :, 4 - i], s_st2.at[dz, s, i - 1], r_st2.at[dz, s, i - 1], to)

    for dz in range(2):
        if dz:
            for cp in far_copies:
                cp.wait_recv()
            own = away[0].astype(F32)
            par = away[1].astype(F32)
            sq1_copies = squares(1, own, par)
            scale = scale_of(1, sq1_copies)
            xb[1, 0, 0, 0] = (own * scale * vec[0:1]).astype(BF16)
            xb[1, 0, 1, 0] = (par * scale * vec2[0:1]).astype(BF16)
        for i in (1, 3, 2):
            stage1(dz, i).start()
            stage2(dz, 0, i).start()
    for cp in stu_copies:
        cp.start()

    def pass_on(dz):
        for s in (1, 3, 2):
            stage1(dz, 4 - s).wait_recv()
            for i in (1, 3, 2):
                stage2(dz, s, i).start()

    pass_on(0)

    def rs_copy(k, i):
        return copy(sent1.at[k, run_of(i)], got1.at[k, i - 1], s_rs.at[k, i - 1], r_rs.at[k, i - 1], on_z(i))

    def ag_copy(k, i):
        q = run_of(2) if i == 3 else zl
        return copy(hidden.at[k, q], hidden.at[k, q], s_ag.at[k, i - 1], r_ag.at[k, i - 1], on_z(1 if i == 3 else i))

    def ag_wait(k, i):
        q = run_of(i)
        return copy(hidden.at[k, q], hidden.at[k, q], s_ag.at[k, i - 1], r_ag.at[k, i - 1], on_z(i))

    def p2_copy(dz, e, r):
        to = at((y + r * (1 - dz)) % 4, zh, (x + r * dz) % 4, zl, c)
        return copy(sent2.at[dz, e, r - 1], got2.at[dz, e, r - 1], s_p2.at[dz, e, r - 1], r_p2.at[dz, e, r - 1], to)

    def p3_copy(dz, e):
        to = at((y + e * dz) % 4, zh, (x + e * (1 - dz)) % 4, zl, c)
        return copy(sent3.at[dz, e - 1], got3.at[dz, e - 1], s_p3.at[dz, e - 1], r_p3.at[dz, e - 1], to)

    def place_of(k):
        return pick(k, [n[0] for n in ORDER]), pick(k, [n[1] for n in ORDER])

    def first(k):
        dz, e = place_of(k)

        @pl.when(k == 1)
        def _():
            pass_on(1)

        for r in range(1, 4):
            copy(xb.at[dz, e, :, r], xb.at[dz, e, :, r], s_st2.at[dz, e, 3 - r], r_st2.at[dz, e, 3 - r], partner).wait_recv()

        for t in range(HID // TILE):
            cols = slice(t * TILE, (t + 1) * TILE)
            a = dot(xb[dz, e, 0].reshape(4 * HALF, FEAT), w_in[:, cols])
            a += dot(xb[dz, e, 1].reshape(4 * HALF, FEAT), w_in2[:, cols])
            a = a.reshape(4, HALF, TILE)
            part[k, :, :, cols] = a
            sent1[k, :, :, cols] = a.astype(BF16)
        for i in (3, 2, 1):
            rs_copy(k, i).start()

    def middle(k):
        for i in range(1, 4):
            rs_copy(k, i).wait_recv()
        pre = part[k, zl] + b_in[...].reshape(1, HID)
        pre += (got1[k, 0].astype(F32) + got1[k, 1].astype(F32)) + got1[k, 2].astype(F32)
        hidden[k, zl] = (0.5 * pre * (1.0 + lax.erf(pre * math.sqrt(0.5)))).astype(BF16)
        for i in (2, 1):
            ag_copy(k, i).start()

    def forward(k):
        ag_wait(k, 2).wait_recv()
        ag_copy(k, 3).start()

    def second(k):
        dz, e = place_of(k)
        for i in (1, 3):
            ag_wait(k, i).wait_recv()
        h = hidden[k].reshape(4 * HALF, HID)
        for f, w in enumerate((w_out, w_out2)):
            for t in range(FEAT // TILE):
                cols = slice(t * TILE, (t + 1) * TILE)
                a = dot(h, w[:, cols]).reshape(4, HALF, TILE)
                total[dz, e, f, :, cols] = a[0]
                for r in range(1, 4):
                    sent2[dz, e, r - 1, f, :, cols] = a[r].astype(BF16)
        for r in (2, 1, 3):
            p2_copy(dz, e, r).start()

    def reduce2(k):
        dz, e = place_of(k)
        for r in range(1, 4):
            p2_copy(dz, e, r).wait_recv()
        a = (total[dz, e] + got2[dz, e, 0].astype(F32)) + (got2[dz, e, 1].astype(F32) + got2[dz, e, 2].astype(F32))

        @pl.when(e == 0)
        def _():
            total[dz, 0] = a

        @pl.when(e > 0)
        def _():
            sent3[dz, e - 1] = a.astype(BF16)
            p3_copy(dz, e).start()

    combos = [(i, p) for p in range(2) for i in range(4) if i or p]
    sa_copies = [
        copy(stua.at[0, 0], stua.at[(4 - i) % 4, p], s_sa.at[0, n], r_sa.at[0, n], on_x(i, p))
        for n, (i, p) in enumerate(combos)
    ]
    sa_copies += [
        copy(stq.at[(y + i) % 4], stub.at[(4 - i) % 4, p], s_sa.at[1, n], r_sa.at[1, n], on_y(i, p))
        for n, (i, p) in enumerate(combos)
    ]

    def gather_student():
        for i in range(1, 4):
            q = run_of(i)
            copy(stu.at[q], stu.at[q], s_stu.at[i - 1], r_stu.at[i - 1], on_z(i)).wait_recv()
        stua[0, 0] = stu[...].reshape(HALF, STU).astype(BF16)
        for i in range(4):
            stq[i] = stua[0, 0, :, i * 256 : (i + 1) * 256]
        stub[0, 0] = stq[y]
        for cp in sa_copies:
            cp.start()

    def predict():
        core_copies[4].wait_recv()
        for f, w in enumerate((w_exit, w_exit2)):
            for t in range(FEAT // TILE):
                cols = slice(t * TILE, (t + 1) * TILE)
                pred[f, :, cols] = dot(stua[0, 0], w[:, cols])

    def transpose_student():
        for cp in sa_copies:
            cp.wait_recv()
        stut1[...] = jnp.transpose(stub[...].reshape(8 * HALF, 256).astype(F32)).astype(BF16)
        stut[...] = jnp.transpose(stua[...].reshape(8 * HALF, STU).astype(F32)).astype(BF16).reshape(8, 4, 32, 8 * HALF)

    back = copy(sent4, got4, s_zh.at[2], r_zh.at[2], far)

    def reduce3(dz):
        for e in range(1, 4):
            p3_copy(dz, e).wait_recv()
        a = (total[dz, 0] + got3[dz, 0].astype(F32)) + (got3[dz, 1].astype(F32) + got3[dz, 2].astype(F32))
        if dz:
            sent4[...] = a.astype(BF16)
            back.start()
        else:
            total[0, 0] = a

    core_copies[2].wait_recv()
    core_copies[3].wait_recv()

    def tick(t, carry):
        @pl.when(t < CHUNKS)
        def _():
            first(t)

        @pl.when((t >= LAG1) & (t < CHUNKS + LAG1))
        def _():
            middle(t - LAG1)

        @pl.when((t >= LAGF) & (t < CHUNKS + LAGF))
        def _():
            forward(t - LAGF)

        @pl.when((t >= LAG2) & (t < CHUNKS + LAG2))
        def _():
            second(t - LAG2)

        @pl.when(t >= LAG3)
        def _():
            reduce2(t - LAG3)

        for when, what in ((2, gather_student), (3, predict), (5, transpose_student)):
            pl.when(t == when)(what)

        @pl.when(t == BACK)
        def _():
            reduce3(1)

        return carry

    lax.fori_loop(0, CHUNKS + LAG3, tick, 0)
    reduce3(0)
    back.wait_recv()
    sq2 = jnp.zeros((HALF, 1), F32)
    for f in range(2):
        v = vec if f == 0 else vec2
        inputs = rows32[:, c].reshape(HALF, FEAT) if f == 0 else take[...].astype(F32)
        a = inputs + (total[0, 0, f] + got4[f].astype(F32)) + v[1:2]
        total[1, 0, f] = a
        sq2 += jnp.sum(a * a, axis=1, keepdims=True)
    sq[8] = jnp.broadcast_to(sq2, (HALF, 128))
    sq2_copies = [copy(sq.at[8], sq.at[8 + i], s_sq.at[2, i - 1], r_sq.at[2, i - 1], on_z(i)) for i in range(1, 4)]
    for cp in sq2_copies:
        cp.start()
    scale = scale_of(2, sq2_copies)
    loss = jnp.zeros((8, 128), F32)
    for f in (1, 0):
        v = vec if f == 0 else vec2
        err = pred[f] - total[1, 0, f] * scale * v[2:3]
        sig[f] = (2.0 * err).astype(BF16)
        for a in range(2):
            sigs[a, f] = sig[f, :, a * SIDE : (a + 1) * SIDE]
        es = jnp.sum((err * err).reshape(4, 8, FEAT), axis=0)
        for t in range(FEAT // 128):
            loss += es[:, t * 128 : (t + 1) * 128]
    for a in range(2):
        siga[a, 0, 0] = sigs[a, 0]

    sig_copies = [
        copy(sigs.at[a, p], siga.at[a, (4 - i) % 4, p], s_sig.at[a, n], r_sig.at[a, n], on_ring(a, i, p))
        for n, (i, p) in enumerate(combos)
        for a in range(2)
    ]
    for cp in sig_copies:
        cp.start()
    l1[zl] = loss
    l1_copies = [copy(l1.at[zl], l1.at[zl], s_l.at[i - 1], r_l.at[i - 1], on_z(i)) for i in range(1, 4)]
    for cp in l1_copies:
        cp.start()

    g = lax.dot_general(sig[0], w_exit[...], (((1,), (1,)), ((), ())), preferred_element_type=F32)
    g += lax.dot_general(sig[1], w_exit2[...], (((1,), (1,)), ((), ())), preferred_element_type=F32)
    gstu[...] = g.reshape(4, 8, STU)
    gs_copies = [
        copy(gstu.at[run_of(i)], gotstu.at[i - 1], s_gs.at[i - 1], r_gs.at[i - 1], on_z(i)) for i in range(1, 4)
    ]
    for cp in gs_copies:
        cp.start()

    for cp in sig_copies:
        cp.wait_recv()
    gexit[0] = dot(stut[:, x].reshape(256, 8 * HALF), siga[0].reshape(8 * HALF, SIDE)).reshape(4, 2, 32, SIDE)
    g = dot(stut1[...], siga[1].reshape(8 * HALF, SIDE)).reshape(2, 4, 32, SIDE)
    for h in range(2):
        gexit[1, :, h] = g[h]
    gy_copies = [
        copy(
            gexit.at[a, ((x if a else y) + i) % 4], gotg.at[a, i - 1], s_gy.at[a, i - 1], r_gy.at[a, i - 1],
            on_ring(1 - a, i),
        )
        for i in range(1, 4)
        for a in range(2)
    ]
    for cp in gy_copies:
        cp.start()

    for i in range(1, 4):
        q = run_of(i)
        copy(l1.at[q], l1.at[q], s_l.at[i - 1], r_l.at[i - 1], on_z(i)).wait_recv()
    l2[x, c] = (l1[0] + l1[1]) + (l1[2] + l1[3])
    l2_copies = [copy(l2.at[x, c], l2.at[x, c], s_l.at[3 + n], r_l.at[3 + n], on_x(i, p)) for n, (i, p) in enumerate(combos)]
    for cp in l2_copies:
        cp.start()
    for cp in gs_copies:
        cp.wait_recv()
    student_out[...] = (gstu[zl] + gotstu[0]) + (gotstu[1] + gotstu[2])
    for n, (i, p) in enumerate(combos):
        xx, cc = (x + 4 - i) % 4, (c + p) % 2
        copy(l2.at[xx, cc], l2.at[xx, cc], s_l.at[3 + n], r_l.at[3 + n], partner).wait_recv()
    l3[y] = jnp.sum(l2[...].reshape(8, 8, 128), axis=0)
    l3_copies = [copy(l3.at[y], l3.at[y], s_l.at[9 + i], r_l.at[9 + i], on_y(i)) for i in range(1, 4)]
    for cp in l3_copies:
        cp.start()
    for cp in gy_copies:
        cp.wait_recv()
    for a in range(2):
        gsum[:, a] = (gexit[a, x if a else y] + gotg[a, 0]) + (gotg[a, 1] + gotg[a, 2])
    gz_copy = copy(gsum.at[1 - zh], gotz, s_gz.at[0], r_gz.at[0], far)
    gz_copy.start()
    for i in range(1, 4):
        yy = (y + 4 - i) % 4
        copy(l3.at[yy], l3.at[yy], s_l.at[9 + i], r_l.at[9 + i], partner).wait_recv()
    l4[zh] = (l3[0] + l3[1]) + (l3[2] + l3[3])
    l4_copy = copy(l4.at[zh], l4.at[zh], s_l.at[13], r_l.at[13], far)
    l4_copy.start()

    for cp in core_copies + stu_copies + sq_copies + sq1_copies + far_copies + [back]:
        cp.wait_send()
    for cp in sa_copies + sq2_copies + sig_copies + l1_copies + gs_copies + gy_copies + l2_copies + l3_copies:
        cp.wait_send()
    for dz in range(2):
        for i in range(1, 4):
            stage1(dz, i).wait_send()
            p3_copy(dz, i).wait_send()

    def drain(k, carry):
        for i in range(1, 4):
            rs_copy(k, i).wait_send()
            ag_copy(k, i).wait_send()
            stage2(k // 4, k % 4, i).wait_send()
            p2_copy(k // 4, k % 4, i).wait_send()
        return carry

    lax.fori_loop(0, CHUNKS, drain, 0)

    copy(l4.at[1 - zh], l4.at[1 - zh], s_l.at[13], r_l.at[13], far).wait_recv()
    loss_out[0, 0] = jnp.sum(l4[0] + l4[1]) / (PATCHES * FEATURES)
    gz_copy.wait_recv()
    for a in range(2):
        exit_out[:, a * SIDE : (a + 1) * SIDE] = (gsum[zh, a] + gotz[a]) / PATCHES
    gz_copy.wait_send()
    l4_copy.wait_send()


def place(a, b, a_out, b_out):
    a_out[...] = a[...]
    b_out[...] = b[...]


def shards(tokens, norm_gain, w_in, b_in, w_out, b_out, out_gain, student, w_exit):
    vm = pltpu.VMEM
    dma = lambda *n: pltpu.SemaphoreType.DMA(n)
    in_vmem = pl.BlockSpec(memory_space=pltpu.VMEM)
    in_hbm = pl.BlockSpec(memory_space=pl.ANY)
    sems = [dma(3)]
    for shape in [(5,), (3, 3), (2, 3), (2, 4, 3), (3,), (CHUNKS, 3), (CHUNKS, 3), (2, 4, 3), (2, 3), (3,), (2, 7), (2, 7), (3,), (2, 3), (1,), (14,)]:
        sems += [dma(*shape), dma(*shape)]
    loss, g_exit, g_student = pl.pallas_call(
        kernel,
        out_shape=(
            jax.ShapeDtypeStruct((1, 1), F32),
            jax.ShapeDtypeStruct((32, FEAT), F32),
            jax.ShapeDtypeStruct((8, STU), F32),
        ),
        in_specs=[in_vmem, in_vmem, in_hbm, in_vmem, in_hbm, in_vmem, in_vmem, in_vmem, in_hbm],
        out_specs=(pl.BlockSpec(memory_space=pltpu.SMEM), in_vmem, in_vmem),
        scratch_shapes=[
            vm((FEAT, HID), BF16),
            vm((HID, FEAT), BF16),
            vm((STU, FEAT), BF16),
            vm((FEAT, HID), BF16),
            vm((HID, FEAT), BF16),
            vm((STU, FEAT), BF16),
            vm((8, FEAT), F32),
            vm((8, FEAT), F32),
            vm((4, 2, 8, FEAT), F32),
            vm((HALF, FEAT), BF16),
            vm((HALF, FEAT), BF16),
            vm((HALF, FEAT), BF16),
            vm((2, HALF, FEAT), BF16),
            vm((12, HALF, 128), F32),
            vm((2, 4, 2, 4, HALF, FEAT), BF16),
            vm((CHUNKS, 4, HALF, HID), F32),
            vm((CHUNKS, 4, HALF, HID), BF16),
            vm((CHUNKS, 3, HALF, HID), BF16),
            vm((CHUNKS, 4, HALF, HID), BF16),
            vm((2, 4, 3, 2, HALF, FEAT), BF16),
            vm((2, 4, 3, 2, HALF, FEAT), BF16),
            vm((2, 4, 2, HALF, FEAT), F32),
            vm((2, 3, 2, HALF, FEAT), BF16),
            vm((2, 3, 2, HALF, FEAT), BF16),
            vm((2, HALF, FEAT), BF16),
            vm((2, HALF, FEAT), BF16),
            vm((4, 8, STU), F32),
            vm((4, HALF, 256), BF16),
            vm((8, 4, 32, 8 * HALF), BF16),
            vm((256, 8 * HALF), BF16),
            vm((4, 2, HALF, STU), BF16),
            vm((4, 2, HALF, 256), BF16),
            vm((2, HALF, FEAT), F32),
            vm((2, HALF, FEAT), BF16),
            vm((2, 2, HALF, SIDE), BF16),
            vm((2, 4, 2, HALF, SIDE), BF16),
            vm((4, 8, STU), F32),
            vm((3, 8, STU), F32),
            vm((2, 4, 2, 32, SIDE), F32),
            vm((2, 3, 2, 32, SIDE), F32),
            vm((2, 2, 32, SIDE), F32),
            vm((2, 32, SIDE), F32),
            vm((4, 8, 128), F32),
            vm((4, 2, 8, 128), F32),
            vm((4, 8, 128), F32),
            vm((2, 8, 128), F32),
        ]
        + sems,
        compiler_params=pltpu.CompilerParams(
            collective_id=0, has_side_effects=True, vmem_limit_bytes=56 * 1024 * 1024
        ),
        name="branch_and_exit",
    )(
        tokens, norm_gain, w_in, b_in, w_out, b_out,
        out_gain, student, w_exit,
    )
    g_exit, g_student = pl.pallas_call(
        place,
        out_shape=(jax.ShapeDtypeStruct((32, FEAT), F32), jax.ShapeDtypeStruct((8, STU), F32)),
        in_specs=[in_vmem] * 2,
        out_specs=(in_vmem, in_vmem),
        name="place",
    )(g_exit, g_student)
    return loss.reshape(()), g_exit, g_student


def solution(mesh):
    placed = (
        P("dp", "mp"),
        P("mp"),
        P("mp", "dp"),
        P("dp"),
        P("dp", "mp"),
        P("mp"),
        P("mp"),
        P(("dp", "mp"), None),
        P(None, "mp"),
    )
    return jax.shard_map(
        shards,
        mesh=mesh,
        in_specs=placed,
        out_specs=(P(), P("dp", "mp"), P(("dp", "mp"), None)),
        check_vma=False,
    )
```

```python
import math

import jax
import jax.numpy as jnp
from jax import lax
from jax.experimental import pallas as pl
from jax.experimental.pallas import tpu as pltpu
from jax.sharding import PartitionSpec as P

EPS = 1e-06
MESH = pl.DeviceIdType.MESH
F32, BF16 = jnp.float32, jnp.bfloat16

ROWS = 64
HALF = 32
FEAT = 768
HID = 768
STU = 1024
FEATURES = 6144
PATCHES = 2048
SIDE = FEAT // 2
TILE = 256
CHUNKS = 8
LAG1, LAGF, LAG2, LAG3 = 1, 2, 3, 4
BACK = 10
ORDER = ((0, 0), (1, 0), (1, 1), (1, 3), (0, 1), (1, 2), (0, 3), (0, 2))


def pick(n, table):
    v = table[0]
    for i in range(1, len(table)):
        v = jnp.where(n >= i, table[i], v)
    return v


def dot(a, b):
    return jnp.dot(a, b, preferred_element_type=F32)


def kernel(
    tokens, norm_gain, w_in_hbm, b_in, w_out_hbm, b_out, out_gain, student, w_exit_hbm,
    loss_out, exit_out, student_out,
    w_in, w_out, w_exit, w_in2, w_out2, w_exit2, vec, vec2, rows32, give, mine, take, away, sq, xb, part, sent1, got1, hidden, sent2, got2,
    total, sent3, got3, sent4, got4, stu, stq, stut, stut1, stua, stub, pred, sig, sigs, siga, gstu, gotstu, gexit, gotg, gsum, gotz,
    l1, l2, l3, l4,
    s_load, s_core, r_core, s_sq, r_sq, s_x0, r_x0, s_st2, r_st2, s_zh, r_zh, s_rs, r_rs, s_ag, r_ag, s_p2, r_p2, s_p3, r_p3,
    s_stu, r_stu, s_sa, r_sa, s_sig, r_sig, s_gs, r_gs, s_gy, r_gy, s_gz, r_gz, s_l, r_l,
):
    d, m = lax.axis_index("dp"), lax.axis_index("mp")
    x, zh, y = d % 4, (d // 4) % 2, d // 8
    zl, c = m // 2, m % 2

    def at(yy, hh, xx, ll, cc):
        return ((yy * 2 + hh) * 4 + xx, ll * 2 + cc)

    def on_x(i, p=0):
        return at(y, zh, (x + i) % 4, zl, (c + p) % 2)

    def on_y(i, p=0):
        return at((y + i) % 4, zh, x, zl, (c + p) % 2)

    def on_ring(a, i, p=0):
        return on_y(i, p) if a else on_x(i, p)

    def run_of(i):
        lo, hi = zl % 2, zl // 2
        lo = (lo + i % 2) % 2
        hi = (hi + i // 2) % 2
        return hi * 2 + lo

    def on_z(i):
        return at(y, zh, x, run_of(i), c)

    far = at(y, 1 - zh, x, zl, c)
    partner = at(y, zh, x, zl, 1 - c)
    far_partner = at(y, 1 - zh, x, zl, 1 - c)

    def copy(src, dst, ss, rs, to):
        return pltpu.make_async_remote_copy(src, dst, ss, rs, device_id=to, device_id_type=MESH)

    bar = pltpu.get_barrier_semaphore()
    peers = [partner, far, far_partner]
    for i in range(1, 4):
        peers += [on_x(i), on_x(i, 1), on_y(i), on_y(i, 1), on_z(i)]
    for p in peers:
        pl.semaphore_signal(bar, 1, device_id=p, device_id_type=MESH)
    loads = [
        pltpu.make_async_copy(src, dst, s_load.at[i])
        for i, (src, dst) in enumerate([(w_in_hbm, w_in), (w_out_hbm, w_out), (w_exit_hbm, w_exit)])
    ]
    for cp in loads:
        cp.start()
    vec[0:1] = norm_gain[...].reshape(1, FEAT)
    vec[1:2] = b_out[...].reshape(1, FEAT)
    vec[2:3] = out_gain[...].reshape(1, FEAT)
    vec[3:8] = jnp.zeros((5, FEAT), F32)
    rows32[...] = tokens[...].astype(F32).reshape(4, 2, 8, FEAT)
    give[...] = rows32[:, 1 - c].reshape(HALF, FEAT).astype(BF16)
    mine[...] = rows32[:, c].reshape(HALF, FEAT).astype(BF16)
    stu[zl] = student[...].astype(F32)
    pl.semaphore_wait(bar, len(peers))

    core_copies = [
        copy(src, dst, s_core.at[i], r_core.at[i], partner)
        for i, (src, dst) in enumerate(
            [(give, take), (vec, vec2), (w_in, w_in2), (w_out, w_out2), (w_exit, w_exit2)]
        )
    ]
    far_copies = [
        copy(mine, away.at[0], s_zh.at[0], r_zh.at[0], far),
        copy(give, away.at[1], s_zh.at[1], r_zh.at[1], far_partner),
    ]
    for cp in core_copies[:2] + far_copies:
        cp.start()
    stu_copies = [copy(stu.at[zl], stu.at[zl], s_stu.at[i - 1], r_stu.at[i - 1], on_z(i)) for i in range(1, 4)]

    def squares(n, u, v):
        sq[4 * n] = jnp.broadcast_to(
            jnp.sum(u * u, axis=1, keepdims=True) + jnp.sum(v * v, axis=1, keepdims=True), (HALF, 128)
        )
        cps = [copy(sq.at[4 * n], sq.at[4 * n + i], s_sq.at[n, i - 1], r_sq.at[n, i - 1], on_z(i)) for i in range(1, 4)]
        for cp in cps:
            cp.start()
        return cps

    def scale_of(n, cps):
        for cp in cps:
            cp.wait_recv()
        ss = (sq[4 * n] + sq[4 * n + 1]) + (sq[4 * n + 2] + sq[4 * n + 3])
        return lax.rsqrt(ss[:, 0:1] / FEATURES + EPS)

    for i in range(3):
        loads[i].wait()
        core_copies[2 + i].start()
    core_copies[0].wait_recv()
    own = rows32[:, c].reshape(HALF, FEAT)
    par = take[...].astype(F32)
    sq_copies = squares(0, own, par)
    core_copies[1].wait_recv()
    scale = scale_of(0, sq_copies)
    xb[0, 0, 0, 0] = (own * scale * vec[0:1]).astype(BF16)
    xb[0, 0, 1, 0] = (par * scale * vec2[0:1]).astype(BF16)

    def stage1(dz, i):
        return copy(xb.at[dz, 0, :, 0], xb.at[dz, 4 - i, :, 0], s_x0.at[dz, i - 1], r_x0.at[dz, i - 1], on_ring(dz, i))

    def stage2(dz, s, i):
        to = at((y + i * (1 - dz)) % 4, zh, (x + i * dz) % 4, zl, c)
        return copy(xb.at[dz, s, :, 0], xb.at[dz, s, :, 4 - i], s_st2.at[dz, s, i - 1], r_st2.at[dz, s, i - 1], to)

    for dz in range(2):
        if dz:
            for cp in far_copies:
                cp.wait_recv()
            own = away[0].astype(F32)
            par = away[1].astype(F32)
            sq1_copies = squares(1, own, par)
            scale = scale_of(1, sq1_copies)
            xb[1, 0, 0, 0] = (own * scale * vec[0:1]).astype(BF16)
            xb[1, 0, 1, 0] = (par * scale * vec2[0:1]).astype(BF16)
        for i in (1, 3, 2):
            stage1(dz, i).start()
            stage2(dz, 0, i).start()
    for cp in stu_copies:
        cp.start()

    def pass_on(dz):
        for s in (1, 3, 2):
            stage1(dz, 4 - s).wait_recv()
            for i in (1, 3, 2):
                stage2(dz, s, i).start()

    pass_on(0)

    def rs_copy(k, i):
        return copy(sent1.at[k, run_of(i)], got1.at[k, i - 1], s_rs.at[k, i - 1], r_rs.at[k, i - 1], on_z(i))

    def ag_copy(k, i):
        q = run_of(2) if i == 3 else zl
        return copy(hidden.at[k, q], hidden.at[k, q], s_ag.at[k, i - 1], r_ag.at[k, i - 1], on_z(1 if i == 3 else i))

    def ag_wait(k, i):
        q = run_of(i)
        return copy(hidden.at[k, q], hidden.at[k, q], s_ag.at[k, i - 1], r_ag.at[k, i - 1], on_z(i))

    def p2_copy(dz, e, r):
        to = at((y + r * (1 - dz)) % 4, zh, (x + r * dz) % 4, zl, c)
        return copy(sent2.at[dz, e, r - 1], got2.at[dz, e, r - 1], s_p2.at[dz, e, r - 1], r_p2.at[dz, e, r - 1], to)

    def p3_copy(dz, e):
        to = at((y + e * dz) % 4, zh, (x + e * (1 - dz)) % 4, zl, c)
        return copy(sent3.at[dz, e - 1], got3.at[dz, e - 1], s_p3.at[dz, e - 1], r_p3.at[dz, e - 1], to)

    def place_of(k):
        return pick(k, [n[0] for n in ORDER]), pick(k, [n[1] for n in ORDER])

    def first(k):
        dz, e = place_of(k)

        @pl.when(k == 1)
        def _():
            pass_on(1)

        for r in range(1, 4):
            copy(xb.at[dz, e, :, r], xb.at[dz, e, :, r], s_st2.at[dz, e, 3 - r], r_st2.at[dz, e, 3 - r], partner).wait_recv()

        for t in range(HID // TILE):
            cols = slice(t * TILE, (t + 1) * TILE)
            a = dot(xb[dz, e, 0].reshape(4 * HALF, FEAT), w_in[:, cols])
            a += dot(xb[dz, e, 1].reshape(4 * HALF, FEAT), w_in2[:, cols])
            a = a.reshape(4, HALF, TILE)
            part[k, :, :, cols] = a
            sent1[k, :, :, cols] = a.astype(BF16)
        for i in (3, 2, 1):
            rs_copy(k, i).start()

    def middle(k):
        for i in range(1, 4):
            rs_copy(k, i).wait_recv()
        pre = part[k, zl] + b_in[...].reshape(1, HID)
        pre += (got1[k, 0].astype(F32) + got1[k, 1].astype(F32)) + got1[k, 2].astype(F32)
        hidden[k, zl] = (0.5 * pre * (1.0 + lax.erf(pre * math.sqrt(0.5)))).astype(BF16)
        for i in (1, 2):
            ag_copy(k, i).start()

    def forward(k):
        ag_wait(k, 2).wait_recv()
        ag_copy(k, 3).start()

    def second(k):
        dz, e = place_of(k)
        for i in (1, 3):
            ag_wait(k, i).wait_recv()
        h = hidden[k].reshape(4 * HALF, HID)
        for f, w in enumerate((w_out, w_out2)):
            for t in range(FEAT // TILE):
                cols = slice(t * TILE, (t + 1) * TILE)
                a = dot(h, w[:, cols]).reshape(4, HALF, TILE)
                total[dz, e, f, :, cols] = a[0]
                for r in range(1, 4):
                    sent2[dz, e, r - 1, f, :, cols] = a[r].astype(BF16)
        for r in (2, 1, 3):
            p2_copy(dz, e, r).start()

    def reduce2(k):
        dz, e = place_of(k)
        for r in range(1, 4):
            p2_copy(dz, e, r).wait_recv()
        a = (total[dz, e] + got2[dz, e, 0].astype(F32)) + (got2[dz, e, 1].astype(F32) + got2[dz, e, 2].astype(F32))

        @pl.when(e == 0)
        def _():
            total[dz, 0] = a

        @pl.when(e > 0)
        def _():
            sent3[dz, e - 1] = a.astype(BF16)
            p3_copy(dz, e).start()

    combos = [(i, p) for p in range(2) for i in range(4) if i or p]
    sa_copies = [
        copy(stua.at[0, 0], stua.at[(4 - i) % 4, p], s_sa.at[0, n], r_sa.at[0, n], on_x(i, p))
        for n, (i, p) in enumerate(combos)
    ]
    sa_copies += [
        copy(stq.at[(y + i) % 4], stub.at[(4 - i) % 4, p], s_sa.at[1, n], r_sa.at[1, n], on_y(i, p))
        for n, (i, p) in enumerate(combos)
    ]

    def gather_student():
        for i in range(1, 4):
            q = run_of(i)
            copy(stu.at[q], stu.at[q], s_stu.at[i - 1], r_stu.at[i - 1], on_z(i)).wait_recv()
        stua[0, 0] = stu[...].reshape(HALF, STU).astype(BF16)
        for i in range(4):
            stq[i] = stua[0, 0, :, i * 256 : (i + 1) * 256]
        stub[0, 0] = stq[y]
        for cp in sa_copies:
            cp.start()

    def predict():
        core_copies[4].wait_recv()
        for f, w in enumerate((w_exit, w_exit2)):
            for t in range(FEAT // TILE):
                cols = slice(t * TILE, (t + 1) * TILE)
                pred[f, :, cols] = dot(stua[0, 0], w[:, cols])

    def transpose_student():
        for cp in sa_copies:
            cp.wait_recv()
        stut1[...] = jnp.transpose(stub[...].reshape(8 * HALF, 256).astype(F32)).astype(BF16)
        stut[...] = jnp.transpose(stua[...].reshape(8 * HALF, STU).astype(F32)).astype(BF16).reshape(8, 4, 32, 8 * HALF)

    back = copy(sent4, got4, s_zh.at[2], r_zh.at[2], far)

    def reduce3(dz):
        for e in range(1, 4):
            p3_copy(dz, e).wait_recv()
        a = (total[dz, 0] + got3[dz, 0].astype(F32)) + (got3[dz, 1].astype(F32) + got3[dz, 2].astype(F32))
        if dz:
            sent4[...] = a.astype(BF16)
            back.start()
        else:
            total[0, 0] = a

    core_copies[2].wait_recv()
    core_copies[3].wait_recv()

    def tick(t, carry):
        @pl.when(t < CHUNKS)
        def _():
            first(t)

        @pl.when((t >= LAG1) & (t < CHUNKS + LAG1))
        def _():
            middle(t - LAG1)

        @pl.when((t >= LAGF) & (t < CHUNKS + LAGF))
        def _():
            forward(t - LAGF)

        @pl.when((t >= LAG2) & (t < CHUNKS + LAG2))
        def _():
            second(t - LAG2)

        @pl.when(t >= LAG3)
        def _():
            reduce2(t - LAG3)

        for when, what in ((5, gather_student), (8, predict), (11, transpose_student)):
            pl.when(t == when)(what)

        @pl.when(t == BACK)
        def _():
            reduce3(1)

        return carry

    lax.fori_loop(0, CHUNKS + LAG3, tick, 0)
    reduce3(0)
    back.wait_recv()
    sq2 = jnp.zeros((HALF, 1), F32)
    for f in range(2):
        v = vec if f == 0 else vec2
        inputs = rows32[:, c].reshape(HALF, FEAT) if f == 0 else take[...].astype(F32)
        a = inputs + (total[0, 0, f] + got4[f].astype(F32)) + v[1:2]
        total[1, 0, f] = a
        sq2 += jnp.sum(a * a, axis=1, keepdims=True)
    sq[8] = jnp.broadcast_to(sq2, (HALF, 128))
    sq2_copies = [copy(sq.at[8], sq.at[8 + i], s_sq.at[2, i - 1], r_sq.at[2, i - 1], on_z(i)) for i in range(1, 4)]
    for cp in sq2_copies:
        cp.start()
    scale = scale_of(2, sq2_copies)
    loss = jnp.zeros((8, 128), F32)
    for f in (1, 0):
        v = vec if f == 0 else vec2
        err = pred[f] - total[1, 0, f] * scale * v[2:3]
        sig[f] = (2.0 * err).astype(BF16)
        for a in range(2):
            sigs[a, f] = sig[f, :, a * SIDE : (a + 1) * SIDE]
        es = jnp.sum((err * err).reshape(4, 8, FEAT), axis=0)
        for t in range(FEAT // 128):
            loss += es[:, t * 128 : (t + 1) * 128]
    for a in range(2):
        siga[a, 0, 0] = sigs[a, 0]

    sig_copies = [
        copy(sigs.at[a, p], siga.at[a, (4 - i) % 4, p], s_sig.at[a, n], r_sig.at[a, n], on_ring(a, i, p))
        for n, (i, p) in enumerate(combos)
        for a in range(2)
    ]
    for cp in sig_copies:
        cp.start()
    l1[zl] = loss
    l1_copies = [copy(l1.at[zl], l1.at[zl], s_l.at[i - 1], r_l.at[i - 1], on_z(i)) for i in range(1, 4)]
    for cp in l1_copies:
        cp.start()

    g = lax.dot_general(sig[0], w_exit[...], (((1,), (1,)), ((), ())), preferred_element_type=F32)
    g += lax.dot_general(sig[1], w_exit2[...], (((1,), (1,)), ((), ())), preferred_element_type=F32)
    gstu[...] = g.reshape(4, 8, STU)
    gs_copies = [
        copy(gstu.at[run_of(i)], gotstu.at[i - 1], s_gs.at[i - 1], r_gs.at[i - 1], on_z(i)) for i in range(1, 4)
    ]
    for cp in gs_copies:
        cp.start()

    for cp in sig_copies:
        cp.wait_recv()
    gexit[0] = dot(stut[:, x].reshape(256, 8 * HALF), siga[0].reshape(8 * HALF, SIDE)).reshape(4, 2, 32, SIDE)
    g = dot(stut1[...], siga[1].reshape(8 * HALF, SIDE)).reshape(2, 4, 32, SIDE)
    for h in range(2):
        gexit[1, :, h] = g[h]
    gy_copies = [
        copy(
            gexit.at[a, ((x if a else y) + i) % 4], gotg.at[a, i - 1], s_gy.at[a, i - 1], r_gy.at[a, i - 1],
            on_ring(1 - a, i),
        )
        for i in range(1, 4)
        for a in range(2)
    ]
    for cp in gy_copies:
        cp.start()

    for i in range(1, 4):
        q = run_of(i)
        copy(l1.at[q], l1.at[q], s_l.at[i - 1], r_l.at[i - 1], on_z(i)).wait_recv()
    l2[x, c] = (l1[0] + l1[1]) + (l1[2] + l1[3])
    l2_copies = [copy(l2.at[x, c], l2.at[x, c], s_l.at[3 + n], r_l.at[3 + n], on_x(i, p)) for n, (i, p) in enumerate(combos)]
    for cp in l2_copies:
        cp.start()
    for cp in gs_copies:
        cp.wait_recv()
    student_out[...] = (gstu[zl] + gotstu[0]) + (gotstu[1] + gotstu[2])
    for n, (i, p) in enumerate(combos):
        xx, cc = (x + 4 - i) % 4, (c + p) % 2
        copy(l2.at[xx, cc], l2.at[xx, cc], s_l.at[3 + n], r_l.at[3 + n], partner).wait_recv()
    l3[y] = jnp.sum(l2[...].reshape(8, 8, 128), axis=0)
    l3_copies = [copy(l3.at[y], l3.at[y], s_l.at[9 + i], r_l.at[9 + i], on_y(i)) for i in range(1, 4)]
    for cp in l3_copies:
        cp.start()
    for cp in gy_copies:
        cp.wait_recv()
    for a in range(2):
        gsum[:, a] = (gexit[a, x if a else y] + gotg[a, 0]) + (gotg[a, 1] + gotg[a, 2])
    gz_copy = copy(gsum.at[1 - zh], gotz, s_gz.at[0], r_gz.at[0], far)
    gz_copy.start()
    for i in range(1, 4):
        yy = (y + 4 - i) % 4
        copy(l3.at[yy], l3.at[yy], s_l.at[9 + i], r_l.at[9 + i], partner).wait_recv()
    l4[zh] = (l3[0] + l3[1]) + (l3[2] + l3[3])
    l4_copy = copy(l4.at[zh], l4.at[zh], s_l.at[13], r_l.at[13], far)
    l4_copy.start()

    for cp in core_copies + stu_copies + sq_copies + sq1_copies + far_copies + [back]:
        cp.wait_send()
    for cp in sa_copies + sq2_copies + sig_copies + l1_copies + gs_copies + gy_copies + l2_copies + l3_copies:
        cp.wait_send()
    for dz in range(2):
        for i in range(1, 4):
            stage1(dz, i).wait_send()
            p3_copy(dz, i).wait_send()

    def drain(k, carry):
        for i in range(1, 4):
            rs_copy(k, i).wait_send()
            ag_copy(k, i).wait_send()
            stage2(k // 4, k % 4, i).wait_send()
            p2_copy(k // 4, k % 4, i).wait_send()
        return carry

    lax.fori_loop(0, CHUNKS, drain, 0)

    copy(l4.at[1 - zh], l4.at[1 - zh], s_l.at[13], r_l.at[13], far).wait_recv()
    loss_out[0, 0] = jnp.sum(l4[0] + l4[1]) / (PATCHES * FEATURES)
    gz_copy.wait_recv()
    for a in range(2):
        exit_out[:, a * SIDE : (a + 1) * SIDE] = (gsum[zh, a] + gotz[a]) / PATCHES
    gz_copy.wait_send()
    l4_copy.wait_send()


def place(a, b, a_out, b_out):
    a_out[...] = a[...]
    b_out[...] = b[...]


def shards(tokens, norm_gain, w_in, b_in, w_out, b_out, out_gain, student, w_exit):
    vm = pltpu.VMEM
    dma = lambda *n: pltpu.SemaphoreType.DMA(n)
    in_vmem = pl.BlockSpec(memory_space=pltpu.VMEM)
    in_hbm = pl.BlockSpec(memory_space=pl.ANY)
    sems = [dma(3)]
    for shape in [(5,), (3, 3), (2, 3), (2, 4, 3), (3,), (CHUNKS, 3), (CHUNKS, 3), (2, 4, 3), (2, 3), (3,), (2, 7), (2, 7), (3,), (2, 3), (1,), (14,)]:
        sems += [dma(*shape), dma(*shape)]
    loss, g_exit, g_student = pl.pallas_call(
        kernel,
        out_shape=(
            jax.ShapeDtypeStruct((1, 1), F32),
            jax.ShapeDtypeStruct((32, FEAT), F32),
            jax.ShapeDtypeStruct((8, STU), F32),
        ),
        in_specs=[in_vmem, in_vmem, in_hbm, in_vmem, in_hbm, in_vmem, in_vmem, in_vmem, in_hbm],
        out_specs=(pl.BlockSpec(memory_space=pltpu.SMEM), in_vmem, in_vmem),
        scratch_shapes=[
            vm((FEAT, HID), BF16),
            vm((HID, FEAT), BF16),
            vm((STU, FEAT), BF16),
            vm((FEAT, HID), BF16),
            vm((HID, FEAT), BF16),
            vm((STU, FEAT), BF16),
            vm((8, FEAT), F32),
            vm((8, FEAT), F32),
            vm((4, 2, 8, FEAT), F32),
            vm((HALF, FEAT), BF16),
            vm((HALF, FEAT), BF16),
            vm((HALF, FEAT), BF16),
            vm((2, HALF, FEAT), BF16),
            vm((12, HALF, 128), F32),
            vm((2, 4, 2, 4, HALF, FEAT), BF16),
            vm((CHUNKS, 4, HALF, HID), F32),
            vm((CHUNKS, 4, HALF, HID), BF16),
            vm((CHUNKS, 3, HALF, HID), BF16),
            vm((CHUNKS, 4, HALF, HID), BF16),
            vm((2, 4, 3, 2, HALF, FEAT), BF16),
            vm((2, 4, 3, 2, HALF, FEAT), BF16),
            vm((2, 4, 2, HALF, FEAT), F32),
            vm((2, 3, 2, HALF, FEAT), BF16),
            vm((2, 3, 2, HALF, FEAT), BF16),
            vm((2, HALF, FEAT), BF16),
            vm((2, HALF, FEAT), BF16),
            vm((4, 8, STU), F32),
            vm((4, HALF, 256), BF16),
            vm((8, 4, 32, 8 * HALF), BF16),
            vm((256, 8 * HALF), BF16),
            vm((4, 2, HALF, STU), BF16),
            vm((4, 2, HALF, 256), BF16),
            vm((2, HALF, FEAT), F32),
            vm((2, HALF, FEAT), BF16),
            vm((2, 2, HALF, SIDE), BF16),
            vm((2, 4, 2, HALF, SIDE), BF16),
            vm((4, 8, STU), F32),
            vm((3, 8, STU), F32),
            vm((2, 4, 2, 32, SIDE), F32),
            vm((2, 3, 2, 32, SIDE), F32),
            vm((2, 2, 32, SIDE), F32),
            vm((2, 32, SIDE), F32),
            vm((4, 8, 128), F32),
            vm((4, 2, 8, 128), F32),
            vm((4, 8, 128), F32),
            vm((2, 8, 128), F32),
        ]
        + sems,
        compiler_params=pltpu.CompilerParams(
            collective_id=0, has_side_effects=True, vmem_limit_bytes=56 * 1024 * 1024
        ),
        name="branch_and_exit",
    )(
        tokens, norm_gain, w_in, b_in, w_out, b_out,
        out_gain, student, w_exit,
    )
    g_exit, g_student = pl.pallas_call(
        place,
        out_shape=(jax.ShapeDtypeStruct((32, FEAT), F32), jax.ShapeDtypeStruct((8, STU), F32)),
        in_specs=[in_vmem] * 2,
        out_specs=(in_vmem, in_vmem),
        name="place",
    )(g_exit, g_student)
    return loss.reshape(()), g_exit, g_student


def solution(mesh):
    placed = (
        P("dp", "mp"),
        P("mp"),
        P("mp", "dp"),
        P("dp"),
        P("dp", "mp"),
        P("mp"),
        P("mp"),
        P(("dp", "mp"), None),
        P(None, "mp"),
    )
    return jax.shard_map(
        shards,
        mesh=mesh,
        in_specs=placed,
        out_specs=(P(), P("dp", "mp"), P(("dp", "mp"), None)),
        check_vma=False,
    )
```
